128 devices in a mesh: ctx: 8 (over x_lo, y), tp: 16 (over x_hi, z, core).
Axes of the slice: x: 4 (x_hi: 2, x_lo: 2; x = x_hi * 2 + x_lo), y: 4, z: 4, core: 2. Of those that a mesh axis runs over, the one named last changes fastest.
Arguments:
- span_query: bfloat16 [2048, 1536], P('ctx'), may hold values from -24 to 24
- span_latent: bfloat16 [2048, 576], P('ctx'), may hold values from -24 to 24
- query_up: bfloat16 [1536, 24576], P(None, 'tp'), may hold values from -0.15625 to 0.15625
- key_value_up: bfloat16 [512, 32768], P(None, 'tp'), may hold values from -0.25 to 0.25
- out_weight: bfloat16 [16384, 7168], P('tp'), may hold values from -0.046875 to 0.046875
- owner_rows: int32 [2048], P('ctx'), may hold values from 0 to 63, as said below
- step_query: bfloat16 [64, 1536], P('ctx'), may hold values from -24 to 24
- latent_cache: bfloat16 [64, 512, 576], P('ctx', 'tp'), may hold values from -24 to 24
- cache_lengths: int32 [64], P('ctx'), may hold values from 1 to 512
Outputs:
- span_output: float32 [2048, 7168], P(('ctx', 'tp'))
- step_output: float32 [64, 16384], P('ctx', 'tp')
The draws below stay inside these ranges and needn't reach their ends.
Inputs may be any that keep to these rules, and one draw needn't show every extreme that they name: `owner_rows`: in every aligned block of 16 tokens at most 4 name rows of one group of 8 consecutive rows, and some group is named by exactly 4 of them.
All inputs are finite; a program needn't handle non-finite values.
Results may differ from the reference program's by a relative error of at most 0.012.
The reference program's roundings to bfloat16 on the way count: a program that leaves them out, or rounds other values in their place, can miss the bound.
Values may be sent and summed in bfloat16 or wider, within the bound.
A program may use at most 192 MiB of HBM per device.

```python
import jax
import jax.numpy as jnp
from jax import lax

D = 7168
QL = 1536
KL = 512
RD = 64
NOPE = 128
VD = 128
HEADS = 128
SPAN = 2048
SUB = 16
CAP = 4
B_DEV = 8
ROWS = 64
LCACHE = 512
N_CTX = 8


def drawn_normal(key, shape):
    return jnp.clip(jax.random.normal(key, shape, jnp.float32), -5.0, 5.0)


def draw_span_query(key, part):
    key = jax.random.fold_in(key, 1)
    values = drawn_normal(key, (SPAN, QL))
    return values.astype(jnp.bfloat16)


def draw_span_latent(key, part):
    key = jax.random.fold_in(key, 2)
    values = drawn_normal(key, (SPAN, KL + RD))
    return values.astype(jnp.bfloat16)


def draw_step_query(key, part):
    key = jax.random.fold_in(key, 3)
    values = drawn_normal(key, (ROWS, QL))
    return values.astype(jnp.bfloat16)


def draw_latent_cache(key, part):
    key = jax.random.fold_in(key, 4)
    values = drawn_normal(key, (ROWS, LCACHE, KL + RD))
    return values.astype(jnp.bfloat16)


def draw_owner_rows(key, part):
    key = jax.random.fold_in(key, 7)
    first, third, fourth = jax.random.split(key, 3)
    blocks = SPAN // SUB
    group_ids = jnp.arange(N_CTX, dtype=jnp.int32)[None, :]
    group_rank = jax.random.randint(first, (blocks, N_CTX), 0, 1 << 20) * N_CTX + group_ids
    picked = jnp.argsort(group_rank, axis=1)[:, :4].astype(jnp.int32)
    slots = jnp.arange(SUB, dtype=jnp.int32)[None, :]
    which = jnp.broadcast_to(slots // CAP, (blocks, SUB))
    groups = jnp.take_along_axis(picked, which, axis=1)
    ranking = jax.random.randint(third, (blocks, SUB), 0, 1 << 20) * SUB + slots
    order = jnp.argsort(ranking, axis=1)
    groups = jnp.take_along_axis(groups, order, axis=1)
    within = jax.random.randint(fourth, (blocks, SUB), 0, B_DEV)
    return (groups * B_DEV + within).reshape(SPAN).astype(jnp.int32)


def draw_cache_lengths(key, part):
    key = jax.random.fold_in(key, 8)
    first, second = jax.random.split(key, 2)
    lengths = jax.random.randint(first, (ROWS,), 1, LCACHE + 1)
    longest = jax.random.randint(second, (), 0, ROWS)
    return jnp.where(jnp.arange(ROWS) == longest, LCACHE, lengths).astype(jnp.int32)


def shard_levels(own_key, shape, shards, least, largest):
    def one(dim, blocks):
        steps = jax.random.uniform(jax.random.fold_in(jax.random.fold_in(own_key, 6), dim), (blocks,), jnp.float32, least / len(shards), largest / len(shards))
        return jnp.repeat(jnp.exp(steps), shape[dim] // blocks).reshape((-1,) + (1,) * (len(shape) - dim - 1))

    factor_of = one(*shards[0])
    for cut in shards[1:]:
        factor_of = factor_of * one(*cut)
    return factor_of


def scatter_about(stream_key, dims, scale, limit, cuts=(), held_as=jnp.bfloat16):
    values = scale * jax.random.normal(stream_key, dims, jnp.float32)
    if cuts:
        values = values * shard_levels(stream_key, dims, cuts, -0.22, 0.18)
    return jnp.clip(values, -limit, limit).astype(held_as)


def setup_inputs(seed: int = 0) -> dict:
    key_of = jax.random.split(jax.random.key(seed), 10)
    return {
        "span_query": draw_span_query(jax.random.fold_in(key_of[9], 71), 0),
        "span_latent": draw_span_latent(jax.random.fold_in(key_of[9], 71), 0),
        "query_up": scatter_about(key_of[2], (QL, HEADS * (NOPE + RD)), QL ** -0.5, 0.15625, ((1, 16),)),
        "key_value_up": scatter_about(key_of[3], (KL, HEADS * (NOPE + VD)), KL ** -0.5, 0.25, ((1, 16),)),
        "out_weight": scatter_about(key_of[4], (HEADS * VD, D), (HEADS * VD) ** -0.5, 0.046875, ((0, 16),)),
        "owner_rows": draw_owner_rows(jax.random.fold_in(key_of[9], 71), 0),
        "step_query": draw_step_query(jax.random.fold_in(key_of[9], 71), 0),
        "latent_cache": draw_latent_cache(jax.random.fold_in(key_of[9], 71), 0),
        "cache_lengths": draw_cache_lengths(jax.random.fold_in(key_of[9], 71), 0),
    }


NEGATIVE = -1e30


def reference(span_query, span_latent, query_up, key_value_up, out_weight, owner_rows, step_query, latent_cache, cache_lengths):
    score_scale = (NOPE + RD) ** -0.5
    queries = jnp.dot(span_query, query_up, preferred_element_type=jnp.float32).astype(jnp.bfloat16).reshape(SPAN, HEADS, NOPE + RD)
    keyval = jnp.dot(span_latent[:, :KL], key_value_up, preferred_element_type=jnp.float32).astype(jnp.bfloat16).reshape(SPAN, HEADS, NOPE + VD)
    key_rope = span_latent[:, KL:]
    positions = jnp.arange(SPAN, dtype=jnp.int32)
    visible = positions[:, None] >= positions[None, :]

    def one_head(head_index):
        head_query = lax.dynamic_index_in_dim(queries, head_index, 1, keepdims=False)
        head_keyval = lax.dynamic_index_in_dim(keyval, head_index, 1, keepdims=False)
        scores = jnp.dot(head_query[:, :NOPE], head_keyval[:, :NOPE].T, preferred_element_type=jnp.float32)
        scores = scores + jnp.dot(head_query[:, NOPE:], key_rope.T, preferred_element_type=jnp.float32)
        scores = jnp.where(visible, scores * score_scale, NEGATIVE)
        row_max = jnp.max(scores, axis=1, keepdims=True)
        raised = jnp.where(visible, jnp.exp(scores - row_max), 0.0)
        row_sum = jnp.sum(raised, axis=1, keepdims=True)
        summed = jnp.dot(raised.astype(jnp.bfloat16), head_keyval[:, NOPE:], preferred_element_type=jnp.float32)
        return (summed / row_sum).astype(jnp.bfloat16)

    head_out = lax.map(one_head, jnp.arange(HEADS, dtype=jnp.int32))
    head_out = jnp.transpose(head_out, (1, 0, 2)).reshape(SPAN, HEADS * VD)
    span_output = jnp.dot(head_out, out_weight, preferred_element_type=jnp.float32)

    step_heads = jnp.dot(step_query, query_up, preferred_element_type=jnp.float32).astype(jnp.bfloat16).reshape(ROWS, HEADS, NOPE + RD)
    up_key = key_value_up.reshape(KL, HEADS, NOPE + VD)
    absorbed = jnp.einsum("rhc,khc->rhk", step_heads[..., :NOPE].astype(jnp.float32), up_key[..., :NOPE].astype(jnp.float32))
    step_key = jnp.concatenate([absorbed.astype(jnp.bfloat16), step_heads[..., NOPE:]], axis=-1)
    step_key = lax.optimization_barrier(step_key).astype(jnp.float32)
    cache_pos = jnp.arange(LCACHE, dtype=jnp.int32)
    cache_seen = cache_pos[None, :] < cache_lengths[:, None]
    cache_scores = jnp.einsum("rhk,rpk->rhp", step_key, latent_cache.astype(jnp.float32)) * score_scale
    cache_scores = jnp.where(cache_seen[:, None, :], cache_scores, NEGATIVE)
    extra_seen = owner_rows[None, :] == jnp.arange(ROWS, dtype=jnp.int32)[:, None]
    extra_scores = jnp.einsum("rhk,tk->rht", step_key, span_latent.astype(jnp.float32)) * score_scale
    extra_scores = jnp.where(extra_seen[:, None, :], extra_scores, NEGATIVE)
    row_max = jnp.maximum(jnp.max(cache_scores, axis=-1), jnp.max(extra_scores, axis=-1))
    cache_raise = jnp.where(cache_seen[:, None, :], jnp.exp(cache_scores - row_max[..., None]), 0.0)
    extra_raise = jnp.where(extra_seen[:, None, :], jnp.exp(extra_scores - row_max[..., None]), 0.0)
    row_sum = jnp.sum(cache_raise, axis=-1) + jnp.sum(extra_raise, axis=-1)
    cache_weights = lax.optimization_barrier(cache_raise.astype(jnp.bfloat16)).astype(jnp.float32)
    extra_weights = lax.optimization_barrier(extra_raise.astype(jnp.bfloat16)).astype(jnp.float32)
    mixed_acc = jnp.einsum("rhp,rpk->rhk", cache_weights, latent_cache[..., :KL].astype(jnp.float32))
    mixed_acc = mixed_acc + jnp.einsum("rht,tk->rhk", extra_weights, span_latent[:, :KL].astype(jnp.float32))
    mixed = (mixed_acc / row_sum[..., None]).astype(jnp.bfloat16)
    mixed = lax.optimization_barrier(mixed).astype(jnp.float32)
    step_output = jnp.einsum("rhk,khc->rhc", mixed, up_key[..., NOPE:].astype(jnp.float32))
    step_output = step_output.reshape(ROWS, HEADS * VD)
    return (span_output, step_output)
```

```python
import math

import jax
import jax.numpy as jnp
from jax import lax
from jax.experimental import pallas as pl
from jax.experimental.pallas import tpu as pltpu
from jax.sharding import PartitionSpec as P

KL = 512
RD = 64
NOPE = 128
VD = 128
HD = 8
TOK = 256
LAT = 640
ROWB = 8
CPOS = 32
QL = 1536
D = 7168
NCTX = 8
NTP = 16
CHIPS = 8
NCH = 7
CW = D // NCH
SH = 16
NEGATIVE = -1e30
EXP_SCALE = (NOPE + RD) ** -0.5 * math.log2(math.e)
MESH = pl.DeviceIdType.MESH
F32 = jnp.float32
BF16 = jnp.bfloat16


def dot(a, b):
    return jnp.dot(a, b, preferred_element_type=F32)


def dot_t(a, b):
    return lax.dot_general(a, b, (((1,), (1,)), ((), ())), preferred_element_type=F32)


def iota(shape, dim):
    return lax.broadcasted_iota(jnp.int32, shape, dim)


def split_pair(y):
    rows = y.shape[0]
    low = iota((rows, 128), 1) < 64
    first, middle, last = y[:, :128], y[:, 128:256], y[:, 256:384]
    middle_turned = pltpu.roll(middle, 64, 1)
    last_turned = pltpu.roll(last, 64, 1)
    zero = jnp.zeros_like(first)
    return (
        (first, jnp.where(low, middle, zero)),
        (jnp.where(low, middle_turned, last_turned), jnp.where(low, last_turned, zero)),
    )


def kernel(
    lat_in, xq_in, wq_in, kv_in, wo_in, sq_ref, cache_in, len_ref,
    out_ref, step_ref,
    lat, ext, xq, wq, kvup, wo, cache, q, run_max, run_sum, run_acc, head_out,
    keys, acc_send, acc_recv, ml_send, ml_recv,
    pair_send, own, pair_recv, stage, rs,
    load_sem, wq_sem, wo_sem, xq_sem,
    lat_s, lat_r, rel_s, rel_r, ext_s, ext_r, key_s, key_r,
    acc_s, acc_r, ml_s, ml_r, pair_s, pair_r, rs_s, rs_r,
):
    c = lax.axis_index("ctx")
    t = lax.axis_index("tp")
    core = t % 2
    chip = t // 2
    sibling = {"ctx": c, "tp": t + 1 - 2 * core}

    def remote(src, dst, send, recv, device):
        return pltpu.make_async_remote_copy(
            src_ref=src, dst_ref=dst, send_sem=send, recv_sem=recv, device_id=device, device_id_type=MESH
        )

    barrier = pltpu.get_barrier_semaphore()
    for d in range(1, NCTX):
        pl.semaphore_signal(barrier, inc=1, device_id={"ctx": (c + d) % NCTX, "tp": t}, device_id_type=MESH)
    for d in range(1, NTP):
        pl.semaphore_signal(barrier, inc=1, device_id={"ctx": c, "tp": (t + d) % NTP}, device_id_type=MESH)

    lat_load = pltpu.make_async_copy(lat_in, lat.at[c], load_sem.at[0])
    lat_load.start()
    wq_loads = [
        pltpu.make_async_copy(wq_in.at[:, pl.ds(768 * n, 768)], wq.at[n], wq_sem.at[n]) for n in range(2)
    ]
    for load in wq_loads:
        load.start()
    kv_load = pltpu.make_async_copy(kv_in, kvup, load_sem.at[1])
    kv_load.start()
    xq_loads = []
    for part in range(2):
        for n in range(CHIPS):
            parity = 1 - core if part == 0 else core
            row = pl.multiple_of((2 * n + parity) * SH, SH)
            xq_loads.append(
                pltpu.make_async_copy(
                    xq_in.at[pl.ds(row, SH)], xq.at[pl.ds((part * CHIPS + n) * SH, SH)], xq_sem.at[part * CHIPS + n]
                )
            )
    for load in xq_loads:
        load.start()
    cache_load = pltpu.make_async_copy(cache_in, cache, load_sem.at[2])
    cache_load.start()

    lat_load.wait()
    pl.semaphore_wait(barrier, NCTX - 1 + NTP - 1)

    half = pl.ds(pl.multiple_of(core * 128, 128), 128)
    other_half = pl.ds(pl.multiple_of((1 - core) * 128, 128), 128)
    handoff = pl.ds(pl.multiple_of(t * SH, SH), SH)

    def lat_copy(source, target):
        return remote(
            lat.at[source, half], lat.at[source, half], lat_s.at[target], lat_r.at[source], {"ctx": target, "tp": t}
        )

    def ext_copy(source, target):
        return remote(lat.at[c, handoff], ext.at[source], ext_s.at[target], ext_r.at[source], {"ctx": target, "tp": t})

    def relay_copy(source):
        return remote(lat.at[source, half], lat.at[source, half], rel_s.at[source], rel_r.at[source], sibling)

    def relay_arrival(source):
        return remote(
            lat.at[source, other_half], lat.at[source, other_half], rel_s.at[source], rel_r.at[source], sibling
        )

    def send_latents(n, carry):
        target = NCTX - 1 - n

        @pl.when(target > c)
        def _():
            lat_copy(c, target).start()

        return carry

    lax.fori_loop(0, NCTX, send_latents, 0)

    def send_handoff(n, carry):
        @pl.when(n != c)
        def _():
            ext_copy(c, n).start()

        return carry

    lax.fori_loop(0, NCTX, send_handoff, 0)
    ext[c] = lat[c, handoff]

    step_query = sq_ref[...]
    nopes, ropes = [], []
    for n in range(2):
        wq_loads[n].wait()
        y = dot(step_query, wq[n]).astype(BF16).astype(F32)
        for m in range(2):
            for nope, rope in split_pair(y[:, 384 * m : 384 * (m + 1)]):
                nopes.append(nope)
                ropes.append(rope)
    kv_load.wait()
    absorbed = jnp.concatenate(
        [dot_t(nopes[h].astype(BF16), kvup[:, 256 * h : 256 * h + 128]) for h in range(HD)], axis=0
    )
    keys[t, :, :KL] = absorbed.astype(BF16)
    keys[t, :, KL:] = jnp.concatenate(ropes, axis=0).astype(BF16)

    def key_copy(other):
        return remote(
            keys.at[t], keys.at[t], key_s.at[other], key_r.at[t], {"ctx": c, "tp": 2 * other + core}
        )

    def key_arrival(other):
        source = 2 * other + core
        return remote(keys.at[source], keys.at[source], key_s.at[other], key_r.at[source], sibling)

    def key_relay(other):
        source = 2 * other + core
        return remote(keys.at[source], keys.at[source], key_s.at[CHIPS + other], key_r.at[source], sibling)

    def key_relay_arrival(other):
        source = 2 * other + 1 - core
        return remote(keys.at[source], keys.at[source], key_s.at[CHIPS + other], key_r.at[source], sibling)

    for d in range(1, CHIPS):
        key_copy((chip + d) % CHIPS).start()
    key_relay(chip).start()

    wo_loads = [
        pltpu.make_async_copy(wo_in.at[:, pl.ds(CW * n, CW)], wo.at[n], wo_sem.at[n]) for n in range(NCH)
    ]
    for load in wo_loads:
        load.start()

    for load in xq_loads:
        load.wait()
    for n in range(2):
        y = dot(xq[...], wq[n])
        for m in range(2):
            for e, (nope, rope) in enumerate(split_pair(y[:, 384 * m : 384 * (m + 1)])):
                q[4 * n + 2 * m + e, :, :128] = nope.astype(BF16)
                q[4 * n + 2 * m + e, :, 128:] = rope.astype(BF16)

    def key_value(block, h):
        kv = dot(lat[block, :, :KL], kvup[:, 256 * h : 256 * (h + 1)]).astype(BF16)
        return jnp.concatenate([kv[:, :128], lat[block, :, KL:]], axis=1), kv[:, 128:]

    row = iota((TOK, TOK), 0)
    parity = jnp.where(row < 128, 1 - core, core)
    position = ((row % 128) // SH) * (2 * SH) + parity * SH + row % SH
    visible = position >= iota((TOK, TOK), 1)
    for h in range(HD):
        key, value = key_value(c, h)
        scores = jnp.where(visible, dot_t(q[h], key), NEGATIVE)
        top = jnp.max(scores, axis=1, keepdims=True)
        raised = jnp.exp2((scores - top) * EXP_SCALE)
        run_max[h] = jnp.broadcast_to(top, (TOK, 128))
        run_sum[h] = raised[:, :128] + raised[:, 128:]
        run_acc[h] = dot(raised.astype(BF16), value)

    def forward(block):
        lat_copy(block, c).wait_recv()
        relay_copy(block).start()

    def fold(block):
        for h in range(HD):
            key, value = key_value(block, h)
            scores = dot_t(q[h], key)
            old = run_max[h]
            top = jnp.maximum(old, jnp.max(scores, axis=1, keepdims=True))
            shrink = jnp.exp2((old - top) * EXP_SCALE)
            raised = jnp.exp2((scores - top[:, :1]) * EXP_SCALE)
            run_max[h] = top
            run_sum[h] = run_sum[h] * shrink + (raised[:, :128] + raised[:, 128:])
            run_acc[h] = run_acc[h] * shrink + dot(raised.astype(BF16), value)

    def relay_keys():
        def one(d, carry):
            other = (chip + d) % CHIPS
            key_arrival(other).wait_recv()
            key_relay(other).start()
            return carry

        lax.fori_loop(1, CHIPS, one, 0)

    def decode():
        def arrivals(n, carry):
            key_relay_arrival(n).wait_recv()

            @pl.when(n != c)
            def _():
                ext_copy(n, c).wait_recv()

            return carry

        lax.fori_loop(0, CHIPS, arrivals, 0)
        cache_load.wait()
        extra = ext[...].reshape(NCTX * SH, LAT)
        column = iota((ROWB, 256), 1)
        length = jnp.zeros((ROWB, 256), jnp.int32)
        for b in range(ROWB):
            length = jnp.where(column // CPOS == b, len_ref[b], length)
        in_cache = (column // CPOS == iota((ROWB, 256), 0)) & (t * CPOS + column % CPOS < length)
        pick = jnp.where(iota((ROWB, 128), 1) == RD, 1.0, 0.0).astype(BF16)
        owner = dot_t(pick, extra[:, KL:])
        named = owner == (ROWB * c + iota((ROWB, 128), 0)).astype(F32)
        bias = jnp.concatenate(
            [jnp.where(in_cache, 0.0, NEGATIVE), jnp.where(named, 0.0, NEGATIVE)], axis=1
        ).astype(F32)
        lane = iota((64, 128), 1)
        sub = iota((64, 128), 0)

        def chunk(g, carry):
            query = keys[pl.ds(4 * g, 4)].reshape(256, LAT)
            scores = jnp.concatenate(
                [
                    dot_t(query[:, :KL], cache[:, :KL]) + dot_t(query[:, KL : KL + RD], cache[:, KL:]),
                    dot_t(query, extra),
                ],
                axis=1,
            )
            scores = (scores.reshape(32, ROWB, 384) * EXP_SCALE + bias[None]).reshape(256, 384)
            top = jnp.max(scores, axis=1, keepdims=True)
            raised = jnp.exp2(scores - top)
            total = jnp.sum(raised, axis=1, keepdims=True)
            weights = raised.astype(BF16)
            mixed = dot(weights[:, :256], cache[:, :KL]) + dot(weights[:, 256:], extra[:, :KL])
            acc_send[pl.ds(4 * g, 4)] = mixed.astype(BF16).reshape(4, 64, KL)
            for n in range(4):
                rows = slice(64 * n, 64 * (n + 1))
                packed = jnp.where(lane == sub, top[rows], 0.0) + jnp.where(lane == sub + 64, total[rows], 0.0)
                ml_send[4 * g + n] = jnp.broadcast_to(jnp.sum(packed, axis=0, keepdims=True), (8, 128))
            return carry

        lax.fori_loop(0, 4, chunk, 0)

        def send(d, carry):
            target = (t + d) % NTP
            acc_copy(target).start()
            ml_copy(target).start()
            return carry

        lax.fori_loop(1, NTP, send, 0)
        acc_recv[t] = acc_send[t]
        ml_recv[t] = ml_send[t]

    def acc_copy(target):
        return remote(
            acc_send.at[target], acc_recv.at[t], acc_s.at[target], acc_r.at[t], {"ctx": c, "tp": target}
        )

    def ml_copy(target):
        return remote(ml_send.at[target], ml_recv.at[t], ml_s.at[target], ml_r.at[t], {"ctx": c, "tp": target})

    def acc_arrival(source):
        return remote(acc_send.at[source], acc_recv.at[source], acc_s.at[source], acc_r.at[source], sibling)

    def ml_arrival(source):
        return remote(ml_send.at[source], ml_recv.at[source], ml_s.at[source], ml_r.at[source], sibling)

    @pl.when(c >= 1)
    def _():
        forward(c - 1)

    def turn(n, carry):
        @pl.when(n < c)
        def _():
            forward(c - n - 1)

        @pl.when(n <= c)
        def _():
            relay_arrival(c - n).wait_recv()
            fold(c - n)

        @pl.when(n == 4)
        def _():
            relay_keys()

        @pl.when(n == 5)
        def _():
            decode()

        return carry

    lax.fori_loop(1, NCTX, turn, 0)

    for h in range(HD):
        total = jnp.sum(run_sum[h], axis=1, keepdims=True)
        head_out[:, 128 * h : 128 * (h + 1)] = (run_acc[h] / total).astype(BF16)

    def pair_copy(n):
        return remote(pair_send.at[n], pair_recv.at[n], pair_s.at[n], pair_r.at[n], sibling)

    def rs_copy(n, other):
        rows = pl.ds(pl.multiple_of(other * SH, SH), SH)
        return remote(
            stage.at[n, rows], rs.at[n, chip], rs_s.at[n, other], rs_r.at[n, chip], {"ctx": c, "tp": 2 * other + core}
        )

    def rs_arrival(n, other):
        rows = pl.ds(pl.multiple_of(other * SH, SH), SH)
        return remote(stage.at[n, rows], rs.at[n, other], rs_s.at[n, other], rs_r.at[n, other], sibling)

    def project(n):
        wo_load = pltpu.make_async_copy(wo_in.at[:, pl.ds(CW * n, CW)], wo.at[n], wo_sem.at[n])
        wo_load.wait()
        for m in range(CW // 256):
            columns = slice(256 * m, 256 * (m + 1))
            y = dot(head_out[...], wo[n, :, columns])
            pair_send[n, :, columns] = y[:128].astype(BF16)
            own[n, :, columns] = y[128:].astype(BF16)
        pair_copy(n).start()

    def spread(n):
        pair_copy(n).wait_recv()
        stage[n] = (own[n].astype(F32) + pair_recv[n].astype(F32)).astype(BF16)

        def one(d, carry):
            rs_copy(n, (chip + d) % CHIPS).start()
            return carry

        lax.fori_loop(1, CHIPS, one, 0)
        rs[n, chip] = stage[n, pl.ds(pl.multiple_of(chip * SH, SH), SH)]

    def column_turn(n, carry):
        @pl.when(n < NCH)
        def _():
            project(n)

        @pl.when(n >= 1)
        def _():
            spread(n - 1)

        return carry

    lax.fori_loop(0, NCH + 1, column_turn, 0)

    def merge_arrivals(d, carry):
        source = (t + d) % NTP
        acc_arrival(source).wait_recv()
        ml_arrival(source).wait_recv()
        return carry

    lax.fori_loop(1, NTP, merge_arrivals, 0)
    lane = iota((64, 128), 1)
    sub = iota((64, 128), 0)
    tops, totals = [], []
    for s in range(NTP):
        packed = jnp.broadcast_to(ml_recv[s, 0:1, :], (64, 128))
        tops.append(jnp.sum(jnp.where(lane == sub, packed, 0.0), axis=1, keepdims=True))
        totals.append(jnp.sum(jnp.where(lane == sub + 64, packed, 0.0), axis=1, keepdims=True))
    top = tops[0]
    for s in range(1, NTP):
        top = jnp.maximum(top, tops[s])
    total = jnp.zeros((64, 1), F32)
    summed = jnp.zeros((64, KL), F32)
    for s in range(NTP):
        weight = jnp.exp2(tops[s] - top)
        total = total + totals[s] * weight
        summed = summed + acc_recv[s].astype(F32) * weight
    mixed = summed / total
    for h in range(HD):
        step_ref[:, 128 * h : 128 * (h + 1)] = dot(
            mixed[ROWB * h : ROWB * (h + 1)].astype(BF16), kvup[:, 256 * h + 128 : 256 * (h + 1)]
        )

    for n in range(NCH):

        def arrive(d, carry, n=n):
            rs_arrival(n, (chip + d) % CHIPS).wait_recv()
            return carry

        lax.fori_loop(1, CHIPS, arrive, 0)
        summed = rs[n, 0].astype(F32)
        for s in range(1, CHIPS):
            summed = summed + rs[n, s].astype(F32)
        out_ref[:, CW * n : CW * (n + 1)] = summed

    def drain_ctx(n, carry):
        @pl.when(n > c)
        def _():
            lat_copy(c, n).wait_send()

        @pl.when(n < c)
        def _():
            relay_copy(n).wait_send()

        @pl.when(n != c)
        def _():
            ext_copy(c, n).wait_send()

        @pl.when(n != chip)
        def _():
            key_copy(n).wait_send()

        key_relay(n).wait_send()
        return carry

    lax.fori_loop(0, NCTX, drain_ctx, 0)

    def drain_tp(d, carry):
        target = (t + d) % NTP
        acc_copy(target).wait_send()
        ml_copy(target).wait_send()
        return carry

    lax.fori_loop(1, NTP, drain_tp, 0)

    def drain_columns(n, carry):
        pair_copy(n).wait_send()

        def one(d, carry):
            rs_copy(n, (chip + d) % CHIPS).wait_send()
            return carry

        return lax.fori_loop(1, CHIPS, one, carry)

    lax.fori_loop(0, NCH, drain_columns, 0)


def body(
    span_query,
    span_latent,
    query_up,
    key_value_up,
    out_weight,
    owner_rows,
    step_query,
    latent_cache,
    cache_lengths,
):
    latent = jnp.concatenate(
        [span_latent, owner_rows[:, None].astype(BF16), jnp.zeros((TOK, LAT - KL - RD - 1), BF16)], axis=1
    )
    dma = pltpu.SemaphoreType.DMA
    vmem = pltpu.VMEM
    anywhere = pl.BlockSpec(memory_space=pl.ANY)
    in_vmem = pl.BlockSpec(memory_space=pltpu.VMEM)
    return pl.pallas_call(
        kernel,
        out_shape=(
            jax.ShapeDtypeStruct((SH, D), F32),
            jax.ShapeDtypeStruct((ROWB, HD * VD), F32),
        ),
        in_specs=[anywhere] * 5 + [in_vmem, anywhere, pl.BlockSpec(memory_space=pltpu.SMEM)],
        out_specs=(in_vmem, in_vmem),
        scratch_shapes=[
            vmem((NCTX, TOK, LAT), BF16),
            vmem((NCTX, SH, LAT), BF16),
            vmem((TOK, QL), BF16),
            vmem((2, QL, 768), BF16),
            vmem((KL, HD * 256), BF16),
            vmem((NCH, HD * VD, CW), BF16),
            vmem((ROWB * CPOS, KL + RD), BF16),
            vmem((HD, TOK, 256), BF16),
            vmem((HD, TOK, 128), F32),
            vmem((HD, TOK, 128), F32),
            vmem((HD, TOK, VD), F32),
            vmem((TOK, HD * VD), BF16),
            vmem((NTP, 64, LAT), BF16),
            vmem((NTP, 64, KL), BF16),
            vmem((NTP, 64, KL), BF16),
            vmem((NTP, 8, 128), F32),
            vmem((NTP, 8, 128), F32),
            vmem((NCH, 128, CW), BF16),
            vmem((NCH, 128, CW), BF16),
            vmem((NCH, 128, CW), BF16),
            vmem((NCH, 128, CW), BF16),
            vmem((NCH, CHIPS, SH, CW), BF16),
            dma((3,)),
            dma((2,)),
            dma((NCH,)),
            dma((2 * CHIPS,)),
            dma((NCTX,)),
            dma((NCTX,)),
            dma((NCTX,)),
            dma((NCTX,)),
            dma((NCTX,)),
            dma((NCTX,)),
            dma((2 * CHIPS,)),
            dma((NTP,)),
            dma((NTP,)),
            dma((NTP,)),
            dma((NTP,)),
            dma((NTP,)),
            dma((NCH,)),
            dma((NCH,)),
            dma((NCH, CHIPS)),
            dma((NCH, CHIPS)),
        ],
        compiler_params=pltpu.CompilerParams(
            collective_id=0, has_side_effects=True, vmem_limit_bytes=60 * 1024 * 1024
        ),
        name="attention",
    )(
        latent,
        span_query,
        query_up,
        key_value_up,
        out_weight,
        step_query,
        latent_cache.reshape(ROWB * CPOS, KL + RD),
        cache_lengths,
    )


def solution(mesh):
    in_specs = (
        P("ctx", None),
        P("ctx", None),
        P(None, "tp"),
        P(None, "tp"),
        P("tp", None),
        P("ctx"),
        P("ctx", None),
        P("ctx", "tp", None),
        P("ctx"),
    )
    out_specs = (P(("ctx", "tp"), None), P("ctx", "tp"))
    return jax.shard_map(body, mesh=mesh, in_specs=in_specs, out_specs=out_specs, check_vma=False)
```

```python
import math

import jax
import jax.numpy as jnp
from jax import lax
from jax.experimental import pallas as pl
from jax.experimental.pallas import tpu as pltpu
from jax.sharding import PartitionSpec as P

KL = 512
RD = 64
NOPE = 128
VD = 128
HD = 8
TOK = 256
LAT = 640
ROWB = 8
CPOS = 32
QL = 1536
D = 7168
NCTX = 8
NTP = 16
CHIPS = 8
NCH = 7
CW = D // NCH
SH = 16
NEGATIVE = -1e30
EXP_SCALE = (NOPE + RD) ** -0.5 * math.log2(math.e)
MESH = pl.DeviceIdType.MESH
F32 = jnp.float32
BF16 = jnp.bfloat16


def dot(a, b):
    return jnp.dot(a, b, preferred_element_type=F32)


def dot_t(a, b):
    return lax.dot_general(a, b, (((1,), (1,)), ((), ())), preferred_element_type=F32)


def iota(shape, dim):
    return lax.broadcasted_iota(jnp.int32, shape, dim)


def split_pair(y):
    rows = y.shape[0]
    low = iota((rows, 128), 1) < 64
    first, middle, last = y[:, :128], y[:, 128:256], y[:, 256:384]
    middle_turned = pltpu.roll(middle, 64, 1)
    last_turned = pltpu.roll(last, 64, 1)
    zero = jnp.zeros_like(first)
    return (
        (first, jnp.where(low, middle, zero)),
        (jnp.where(low, middle_turned, last_turned), jnp.where(low, last_turned, zero)),
    )


def kernel(
    lat_ref, owner_ref, xq_in, wq_in, kv_in, wo_in, sq_ref, cache_in, len_ref,
    out_ref, step_ref,
    lat, ext, xq, wq, wk, wv, wv_t, wo, cache, q, run_max, run_sum, run_acc, head_out,
    keys, acc_send, acc_recv, ml_send, ml_recv,
    pair_send, own, pair_recv, stage, x_recv, x_sum, z_recv,
    load_sem, kv_sem, wq_sem, wo_sem, xq_sem,
    lat_s, lat_r, rel_s, rel_r, ext_s, ext_r, cache_s, cache_r, key_s, key_r,
    acc_s, acc_r, ml_s, ml_r, pair_s, pair_r, x_s, x_r, z_s, z_r,
):
    c = lax.axis_index("ctx")
    t = lax.axis_index("tp")
    core = t % 2
    chip = t // 2
    sibling = {"ctx": c, "tp": t + 1 - 2 * core}
    across = (t + CHIPS) % NTP

    def remote(src, dst, send, recv, device):
        return pltpu.make_async_remote_copy(
            src_ref=src, dst_ref=dst, send_sem=send, recv_sem=recv, device_id=device, device_id_type=MESH
        )

    barrier = pltpu.get_barrier_semaphore()
    for d in range(1, NCTX):
        pl.semaphore_signal(barrier, inc=1, device_id={"ctx": (c + d) % NCTX, "tp": t}, device_id_type=MESH)
    for d in range(NCTX // 2):
        other_row = (c // 4 * 4 + 4) % NCTX + d
        pl.semaphore_signal(barrier, inc=1, device_id={"ctx": other_row, "tp": across}, device_id_type=MESH)
    for d in range(1, CHIPS):
        pl.semaphore_signal(barrier, inc=1, device_id={"ctx": c, "tp": (t + 2 * d) % NTP}, device_id_type=MESH)
    pl.semaphore_signal(barrier, inc=1, device_id=sibling, device_id_type=MESH)

    wq_loads = [
        pltpu.make_async_copy(wq_in.at[:, pl.ds(768 * n, 768)], wq.at[n], wq_sem.at[n]) for n in range(2)
    ]
    for load in wq_loads:
        load.start()
    kv_loads = []
    for h in range(HD):
        for part, held in enumerate((wk, wv)):
            kv_loads.append(
                pltpu.make_async_copy(
                    kv_in.at[:, pl.ds(256 * h + 128 * part, 128)], held.at[:, pl.ds(128 * h, 128)], kv_sem.at[part, h]
                )
            )
    for load in kv_loads:
        load.start()
    xq_loads = []
    for part in range(2):
        for n in range(CHIPS):
            parity = 1 - core if part == 0 else core
            row = pl.multiple_of((2 * n + parity) * SH, SH)
            xq_loads.append(
                pltpu.make_async_copy(
                    xq_in.at[pl.ds(row, SH)], xq.at[pl.ds((part * CHIPS + n) * SH, SH)], xq_sem.at[part * CHIPS + n]
                )
            )
    for load in xq_loads:
        load.start()
    cache_load = pltpu.make_async_copy(cache_in, cache.at[core], load_sem.at[0])
    cache_load.start()

    owner_row = jnp.broadcast_to(owner_ref[...].astype(F32).reshape(1, TOK), (LAT - KL - RD, TOK))
    owner_row = jnp.where(iota((LAT - KL - RD, TOK), 0) == 0, owner_row, 0.0)
    lat[c] = jnp.concatenate([lat_ref[...].astype(F32), owner_row], axis=0).T.astype(BF16)

    pl.semaphore_wait(barrier, NCTX - 1 + NCTX // 2 + CHIPS - 1 + 1)

    half = pl.ds(pl.multiple_of(core * 128, 128), 128)
    other_half = pl.ds(pl.multiple_of((1 - core) * 128, 128), 128)
    quarters = [pl.ds(pl.multiple_of(core * 128 + 64 * n, 64), 64) for n in range(2)]
    handoff = pl.ds(pl.multiple_of(t * SH, SH), SH)

    def lat_copy(source, target, n):
        tp = t if n == 0 else jnp.where(source // 4 == target // 4, t, across)
        return remote(
            lat.at[source, quarters[n]],
            lat.at[source, quarters[n]],
            lat_s.at[n, target],
            lat_r.at[n, source],
            {"ctx": target, "tp": tp},
        )

    def ext_copy(source, target):
        return remote(
            lat.at[c, handoff], ext.at[core, source], ext_s.at[target], ext_r.at[source], {"ctx": target, "tp": t}
        )

    def ext_relay(whose):
        return remote(ext.at[whose], ext.at[whose], ext_s.at[NCTX], ext_r.at[NCTX], sibling)

    def cache_relay(whose):
        return remote(cache.at[whose], cache.at[whose], cache_s, cache_r, sibling)

    def relay_copy(source):
        return remote(lat.at[source, half], lat.at[source, half], rel_s.at[source], rel_r.at[source], sibling)

    def relay_arrival(source):
        return remote(
            lat.at[source, other_half], lat.at[source, other_half], rel_s.at[source], rel_r.at[source], sibling
        )

    def send_latents(n, carry):
        target = NCTX - 1 - n

        @pl.when(target > c)
        def _():
            lat_copy(c, target, 0).start()
            lat_copy(c, target, 1).start()

        return carry

    lax.fori_loop(0, NCTX, send_latents, 0)

    def send_handoff(n, carry):
        @pl.when(n != c)
        def _():
            ext_copy(c, n).start()

        return carry

    lax.fori_loop(0, NCTX, send_handoff, 0)
    ext[core, c] = lat[c, handoff]
    cache_load.wait()
    cache_relay(core).start()

    step_query = sq_ref[...]
    nopes, ropes = [], []
    for n in range(2):
        wq_loads[n].wait()
        y = dot(step_query, wq[n]).astype(BF16).astype(F32)
        for m in range(2):
            for nope, rope in split_pair(y[:, 384 * m : 384 * (m + 1)]):
                nopes.append(nope)
                ropes.append(rope)
    for load in kv_loads:
        load.wait()
    absorbed = jnp.concatenate(
        [dot_t(nopes[h].astype(BF16), wk[:, 128 * h : 128 * (h + 1)]) for h in range(HD)], axis=0
    )
    keys[chip, :, :KL] = absorbed.astype(BF16)
    keys[chip, :, KL:] = jnp.concatenate(ropes, axis=0).astype(BF16)

    def key_copy(other):
        return remote(
            keys.at[chip], keys.at[chip], key_s.at[other], key_r.at[chip], {"ctx": c, "tp": 2 * other + core}
        )

    def key_arrival(other):
        return remote(keys.at[other], keys.at[other], key_s.at[other], key_r.at[other], sibling)

    for d in range(1, CHIPS):
        key_copy((chip + d) % CHIPS).start()

    wo_loads = [
        pltpu.make_async_copy(wo_in.at[:, pl.ds(CW * n, CW)], wo.at[n], wo_sem.at[n]) for n in range(NCH)
    ]
    for load in wo_loads:
        load.start()

    for load in xq_loads:
        load.wait()
    for n in range(2):
        y = dot(xq[...], wq[n])
        for m in range(2):
            for e, (nope, rope) in enumerate(split_pair(y[:, 384 * m : 384 * (m + 1)])):
                q[4 * n + 2 * m + e, :128] = nope.T.astype(BF16)
                q[4 * n + 2 * m + e, 128:] = rope.T.astype(BF16)

    wv_t[...] = wv[...].T

    column = iota((TOK, TOK), 1)
    parity = jnp.where(column < 128, 1 - core, core)
    position = ((column % 128) // SH) * (2 * SH) + parity * SH + column % SH
    visible = iota((TOK, TOK), 0) <= position

    def fold(block, first):
        latents = lat[block, :, :KL]
        rope = lat[block, :, KL:]
        key = dot(latents, wk[...]).astype(BF16)
        value = dot(wv_t[...], latents.T).astype(BF16)

        def score(h):
            return dot(jnp.concatenate([key[:, 128 * h : 128 * (h + 1)], rope], axis=1), q[h])

        def weigh(h, weights, shrink):
            added = dot(value[128 * h : 128 * (h + 1)], weights)
            if not first:
                added = added + (run_acc[h].reshape(VD // 8, 8, TOK) * shrink[None]).reshape(VD, TOK)
            run_acc[h] = added

        scores = {h: score(h) for h in range(2)}
        late = None
        for h in range(HD):
            if h + 2 < HD:
                scores[h + 2] = score(h + 2)
            if late is not None:
                weigh(*late)
            here = scores.pop(h)
            if first:
                here = jnp.where(visible, here, NEGATIVE)
            here = here.reshape(TOK // 8, 8, TOK)
            top = jnp.max(jnp.max(here, axis=0), axis=0, keepdims=True)
            shrink = None
            if first:
                top = jnp.broadcast_to(top, (8, TOK))
            else:
                old = run_max[h]
                top = jnp.maximum(old, top)
                shrink = jnp.exp2((old - top) * EXP_SCALE)
            raised = jnp.exp2((here - top[None]) * EXP_SCALE)
            total = jnp.sum(raised, axis=0)
            run_max[h] = top
            run_sum[h] = total if first else run_sum[h] * shrink + total
            late = (h, raised.reshape(TOK, TOK).astype(BF16), shrink)
        weigh(*late)

    fold(c, True)

    def forward(block):
        lat_copy(block, c, 0).wait_recv()
        lat_copy(block, c, 1).wait_recv()
        relay_copy(block).start()

    def relay_handoff():
        def one(n, carry):
            @pl.when(n != c)
            def _():
                ext_copy(n, c).wait_recv()

            return carry

        lax.fori_loop(0, NCTX, one, 0)
        ext_relay(core).start()

    def decode():
        def arrivals(d, carry):
            key_arrival((chip + d) % CHIPS).wait_recv()
            return carry

        lax.fori_loop(1, CHIPS, arrivals, 0)
        ext_relay(1 - core).wait_recv()
        cache_relay(1 - core).wait_recv()
        extra = ext[...].reshape(2 * NCTX * SH, LAT)
        cached = cache[...].reshape(2 * ROWB * CPOS, KL + RD)
        shape = (ROWB, 512)
        column = iota(shape, 1)
        length = jnp.zeros(shape, jnp.int32)
        for b in range(ROWB):
            length = jnp.where(column % 256 // CPOS == b, len_ref[b], length)
        place = (2 * chip + column // 256) * CPOS + column % CPOS
        in_cache = (column % 256 // CPOS == iota(shape, 0)) & (place < length)
        pick = jnp.where(iota((ROWB, 128), 1) == RD, 1.0, 0.0).astype(BF16)
        owner = dot_t(pick, extra[:, KL:])
        named = owner == (ROWB * c + iota((ROWB, 256), 0)).astype(F32)
        bias = jnp.concatenate(
            [jnp.where(in_cache, 0.0, NEGATIVE), jnp.where(named, 0.0, NEGATIVE)], axis=1
        ).astype(F32)
        lane = iota((64, 128), 1)
        sub = iota((64, 128), 0)

        def chunk(g):
            query = keys[2 * g : 2 * g + 2].reshape(128, LAT)
            scores = jnp.concatenate(
                [
                    dot_t(query[:, :KL], cached[:, :KL]) + dot_t(query[:, KL : KL + RD], cached[:, KL:]),
                    dot_t(query, extra),
                ],
                axis=1,
            )
            scores = (scores.reshape(16, ROWB, 768) * EXP_SCALE + bias[None]).reshape(128, 768)
            top = jnp.max(scores, axis=1, keepdims=True)
            raised = jnp.exp2(scores - top)
            total = jnp.sum(raised, axis=1, keepdims=True)
            weights = raised.astype(BF16)
            mixed = dot(weights[:, :512], cached[:, :KL]) + dot(weights[:, 512:], extra[:, :KL])
            acc_send[2 * g : 2 * g + 2] = mixed.astype(BF16).reshape(2, 64, KL)
            for n in range(2):
                rows = slice(64 * n, 64 * (n + 1))
                packed = jnp.where(lane == sub, top[rows], 0.0) + jnp.where(lane == sub + 64, total[rows], 0.0)
                ml_send[2 * g + n] = jnp.broadcast_to(jnp.sum(packed, axis=0, keepdims=True), (8, 128))

        for g in range(4):
            chunk(g)

        def send(d, carry):
            target = (chip + d) % CHIPS
            acc_copy(target).start()
            ml_copy(target).start()
            return carry

        lax.fori_loop(1, CHIPS, send, 0)
        acc_recv[chip] = acc_send[chip]
        ml_recv[chip] = ml_send[chip]

    def acc_copy(target):
        return remote(
            acc_send.at[target],
            acc_recv.at[chip],
            acc_s.at[target],
            acc_r.at[chip],
            {"ctx": c, "tp": 2 * target + core},
        )

    def ml_copy(target):
        return remote(
            ml_send.at[target], ml_recv.at[chip], ml_s.at[target], ml_r.at[chip], {"ctx": c, "tp": 2 * target + core}
        )

    def acc_arrival(source):
        return remote(acc_send.at[source], acc_recv.at[source], acc_s.at[source], acc_r.at[source], sibling)

    def ml_arrival(source):
        return remote(ml_send.at[source], ml_recv.at[source], ml_s.at[source], ml_r.at[source], sibling)

    @pl.when(c >= 1)
    def _():
        forward(c - 1)

    def turn(n, carry):
        @pl.when(n < c)
        def _():
            forward(c - n - 1)

        @pl.when(n <= c)
        def _():
            relay_arrival(c - n).wait_recv()
            fold(c - n, False)

        @pl.when(n == 4)
        def _():
            relay_handoff()

        @pl.when(n == 5)
        def _():
            decode()

        return carry

    lax.fori_loop(1, NCTX, turn, 0)

    for h in range(HD):
        total = jnp.sum(run_sum[h], axis=0, keepdims=True)
        head_out[:, 128 * h : 128 * (h + 1)] = (run_acc[h] / total).T.astype(BF16)

    def pair_copy(n):
        return remote(pair_send.at[n], pair_recv.at[n], pair_s.at[n], pair_r.at[n], sibling)

    x_hi = chip // 4
    z = chip % 4
    here_rows = pl.ds(pl.multiple_of(x_hi * 64, 64), 64)
    there_rows = pl.ds(pl.multiple_of(64 - x_hi * 64, 64), 64)

    def x_copy(n):
        return remote(stage.at[n, there_rows], x_recv.at[n], x_s.at[n], x_r.at[n], {"ctx": c, "tp": across})

    def z_copy(n, other):
        rows = pl.ds(pl.multiple_of(other * SH, SH), SH)
        return remote(
            x_sum.at[n, rows],
            z_recv.at[n, z],
            z_s.at[n, other],
            z_r.at[n, z],
            {"ctx": c, "tp": 8 * x_hi + 2 * other + core},
        )

    def z_arrival(n, other):
        return remote(z_recv.at[n, other], z_recv.at[n, other], z_s.at[n, other], z_r.at[n, other], sibling)

    def project(n):
        wo_load = pltpu.make_async_copy(wo_in.at[:, pl.ds(CW * n, CW)], wo.at[n], wo_sem.at[n])
        wo_load.wait()
        for m in range(CW // 256):
            columns = slice(256 * m, 256 * (m + 1))
            y = dot(head_out[...], wo[n, :, columns])
            pair_send[n, :, columns] = y[:128].astype(BF16)
            own[n, :, columns] = y[128:].astype(BF16)
        pair_copy(n).start()

    def add_core(n):
        pair_copy(n).wait_recv()
        stage[n] = (own[n].astype(F32) + pair_recv[n].astype(F32)).astype(BF16)
        x_copy(n).start()

    def add_x(n):
        x_copy(n).wait_recv()
        x_sum[n] = (stage[n, here_rows].astype(F32) + x_recv[n].astype(F32)).astype(BF16)
        for d in range(1, 4):
            z_copy(n, (z + d) % 4).start()
        z_recv[n, z] = x_sum[n, pl.ds(pl.multiple_of(z * SH, SH), SH)]

    def column_turn(n, carry):
        @pl.when(n < NCH)
        def _():
            project(n)

        @pl.when((n >= 2) & (n < NCH + 2))
        def _():
            add_core(n - 2)

        @pl.when(n >= 4)
        def _():
            add_x(n - 4)

        return carry

    lax.fori_loop(0, NCH + 4, column_turn, 0)

    def merge_arrivals(d, carry):
        source = (chip + d) % CHIPS
        acc_arrival(source).wait_recv()
        ml_arrival(source).wait_recv()
        return carry

    lax.fori_loop(1, CHIPS, merge_arrivals, 0)
    lane = iota((64, 128), 1)
    sub = iota((64, 128), 0)
    tops, totals = [], []
    for s in range(CHIPS):
        packed = jnp.broadcast_to(ml_recv[s, 0:1, :], (64, 128))
        tops.append(jnp.sum(jnp.where(lane == sub, packed, 0.0), axis=1, keepdims=True))
        totals.append(jnp.sum(jnp.where(lane == sub + 64, packed, 0.0), axis=1, keepdims=True))
    top = tops[0]
    for s in range(1, CHIPS):
        top = jnp.maximum(top, tops[s])
    total = jnp.zeros((64, 1), F32)
    summed = jnp.zeros((64, KL), F32)
    for s in range(CHIPS):
        weight = jnp.exp2(tops[s] - top)
        total = total + totals[s] * weight
        summed = summed + acc_recv[s].astype(F32) * weight
    mixed = summed / total
    for h in range(HD):
        step_ref[:, 128 * h : 128 * (h + 1)] = dot(
            mixed[ROWB * h : ROWB * (h + 1)].astype(BF16), wv[:, 128 * h : 128 * (h + 1)]
        )

    for n in range(NCH):
        for d in range(1, 4):
            z_arrival(n, (z + d) % 4).wait_recv()
        summed = z_recv[n, 0].astype(F32)
        for other in range(1, 4):
            summed = summed + z_recv[n, other].astype(F32)
        out_ref[:, CW * n : CW * (n + 1)] = summed

    def drain_ctx(n, carry):
        @pl.when(n > c)
        def _():
            lat_copy(c, n, 0).wait_send()
            lat_copy(c, n, 1).wait_send()

        @pl.when(n < c)
        def _():
            relay_copy(n).wait_send()

        @pl.when(n != c)
        def _():
            ext_copy(c, n).wait_send()

        @pl.when(n != chip)
        def _():
            key_copy(n).wait_send()
            acc_copy(n).wait_send()
            ml_copy(n).wait_send()

        return carry

    lax.fori_loop(0, NCTX, drain_ctx, 0)

    ext_relay(core).wait_send()
    cache_relay(core).wait_send()

    def drain_columns(n, carry):
        pair_copy(n).wait_send()
        x_copy(n).wait_send()
        for d in range(1, 4):
            z_copy(n, (z + d) % 4).wait_send()
        return carry

    lax.fori_loop(0, NCH, drain_columns, 0)


def body(
    span_query,
    span_latent,
    query_up,
    key_value_up,
    out_weight,
    owner_rows,
    step_query,
    latent_cache,
    cache_lengths,
):
    dma = pltpu.SemaphoreType.DMA
    vmem = pltpu.VMEM
    anywhere = pl.BlockSpec(memory_space=pl.ANY)
    in_vmem = pl.BlockSpec(memory_space=pltpu.VMEM)
    return pl.pallas_call(
        kernel,
        out_shape=(
            jax.ShapeDtypeStruct((SH, D), F32),
            jax.ShapeDtypeStruct((ROWB, HD * VD), F32),
        ),
        in_specs=[in_vmem] * 2 + [anywhere] * 4 + [in_vmem, anywhere, pl.BlockSpec(memory_space=pltpu.SMEM)],
        out_specs=(in_vmem, in_vmem),
        scratch_shapes=[
            vmem((NCTX, TOK, LAT), BF16),
            vmem((2, NCTX, SH, LAT), BF16),
            vmem((TOK, QL), BF16),
            vmem((2, QL, 768), BF16),
            vmem((KL, HD * NOPE), BF16),
            vmem((KL, HD * VD), BF16),
            vmem((HD * VD, KL), BF16),
            vmem((NCH, HD * VD, CW), BF16),
            vmem((2, ROWB * CPOS, KL + RD), BF16),
            vmem((HD, TOK, 256), BF16),
            vmem((HD, 8, TOK), F32),
            vmem((HD, 8, TOK), F32),
            vmem((HD, VD, TOK), F32),
            vmem((TOK, HD * VD), BF16),
            vmem((CHIPS, 64, LAT), BF16),
            vmem((CHIPS, 64, KL), BF16),
            vmem((CHIPS, 64, KL), BF16),
            vmem((CHIPS, 8, 128), F32),
            vmem((CHIPS, 8, 128), F32),
            vmem((NCH, 128, CW), BF16),
            vmem((NCH, 128, CW), BF16),
            vmem((NCH, 128, CW), BF16),
            vmem((NCH, 128, CW), BF16),
            vmem((NCH, 64, CW), BF16),
            vmem((NCH, 64, CW), BF16),
            vmem((NCH, 4, SH, CW), BF16),
            dma((1,)),
            dma((2, HD)),
            dma((2,)),
            dma((NCH,)),
            dma((2 * CHIPS,)),
            dma((2, NCTX)),
            dma((2, NCTX)),
            dma((NCTX,)),
            dma((NCTX,)),
            dma((NCTX + 1,)),
            dma((NCTX + 1,)),
            dma,
            dma,
            dma((CHIPS,)),
            dma((CHIPS,)),
            dma((CHIPS,)),
            dma((CHIPS,)),
            dma((CHIPS,)),
            dma((CHIPS,)),
            dma((NCH,)),
            dma((NCH,)),
            dma((NCH,)),
            dma((NCH,)),
            dma((NCH, 4)),
            dma((NCH, 4)),
        ],
        compiler_params=pltpu.CompilerParams(
            collective_id=0, has_side_effects=True, vmem_limit_bytes=60 * 1024 * 1024
        ),
        name="attention",
    )(
        span_latent.T,
        owner_rows,
        span_query,
        query_up,
        key_value_up,
        out_weight,
        step_query,
        latent_cache.reshape(ROWB * CPOS, KL + RD),
        cache_lengths,
    )


def solution(mesh):
    in_specs = (
        P("ctx", None),
        P("ctx", None),
        P(None, "tp"),
        P(None, "tp"),
        P("tp", None),
        P("ctx"),
        P("ctx", None),
        P("ctx", "tp", None),
        P("ctx"),
    )
    out_specs = (P(("ctx", "tp"), None), P("ctx", "tp"))
    return jax.shard_map(body, mesh=mesh, in_specs=in_specs, out_specs=out_specs, check_vma=False)
```

```python
import math

import jax
import jax.numpy as jnp
from jax import lax
from jax.experimental import pallas as pl
from jax.experimental.pallas import tpu as pltpu
from jax.sharding import PartitionSpec as P

KL = 512
RD = 64
NOPE = 128
VD = 128
HD = 8
TOK = 256
LAT = 640
ROWB = 8
CPOS = 32
QL = 1536
D = 7168
NCTX = 8
NTP = 16
CHIPS = 8
NCH = 7
CW = D // NCH
SH = 16
NEGATIVE = -1e30
EXP_SCALE = (NOPE + RD) ** -0.5 * math.log2(math.e)
MESH = pl.DeviceIdType.MESH
F32 = jnp.float32
BF16 = jnp.bfloat16


def dot(a, b):
    return jnp.dot(a, b, preferred_element_type=F32)


def dot_t(a, b):
    return lax.dot_general(a, b, (((1,), (1,)), ((), ())), preferred_element_type=F32)


def iota(shape, dim):
    return lax.broadcasted_iota(jnp.int32, shape, dim)


def split_pair(y):
    rows = y.shape[0]
    low = iota((rows, 128), 1) < 64
    first, middle, last = y[:, :128], y[:, 128:256], y[:, 256:384]
    middle_turned = pltpu.roll(middle, 64, 1)
    last_turned = pltpu.roll(last, 64, 1)
    zero = jnp.zeros_like(first)
    return (
        (first, jnp.where(low, middle, zero)),
        (jnp.where(low, middle_turned, last_turned), jnp.where(low, last_turned, zero)),
    )


def kernel(
    lat_ref, owner_ref, xq_in, wq_in, kv_in, wo_in, sq_ref, cache_in, len_ref,
    out_ref, step_ref,
    lat, ext, xq, wq, wk, wv, wv_t, wo, cache, q, run_max, run_sum, run_acc, head_out,
    keys, acc_send, acc_recv, ml_send, ml_recv,
    pair_send, own, pair_recv, stage, x_recv, x_sum, z_recv, zz_recv,
    load_sem, kv_sem, wq_sem, wo_sem, xq_sem,
    lat_s, lat_r, over_s, over_r, rel_s, rel_r, ext_s, ext_r, cache_s, cache_r, key_s, key_r,
    acc_s, acc_r, ml_s, ml_r, pair_s, pair_r, x_s, x_r, z_s, z_r,
):
    c = lax.axis_index("ctx")
    t = lax.axis_index("tp")
    core = t % 2
    chip = t // 2
    sibling = {"ctx": c, "tp": t + 1 - 2 * core}
    across = (t + CHIPS) % NTP
    opposite = (chip + 4) % CHIPS
    x_hi = chip // 4
    z = chip % 4
    x_lo = c // 4
    y = c % 4

    def remote(src, dst, send, recv, device):
        return pltpu.make_async_remote_copy(
            src_ref=src, dst_ref=dst, send_sem=send, recv_sem=recv, device_id=device, device_id_type=MESH
        )

    barrier = pltpu.get_barrier_semaphore()
    for d in range(1, NCTX):
        pl.semaphore_signal(barrier, inc=1, device_id={"ctx": (c + d) % NCTX, "tp": t}, device_id_type=MESH)
    pl.semaphore_signal(barrier, inc=1, device_id={"ctx": (c + 4) % NCTX, "tp": across}, device_id_type=MESH)
    for d in range(1, CHIPS):
        pl.semaphore_signal(barrier, inc=1, device_id={"ctx": c, "tp": (t + 2 * d) % NTP}, device_id_type=MESH)
    pl.semaphore_signal(barrier, inc=1, device_id=sibling, device_id_type=MESH)

    wq_loads = [
        pltpu.make_async_copy(wq_in.at[:, pl.ds(768 * n, 768)], wq.at[n], wq_sem.at[n]) for n in range(2)
    ]
    for load in wq_loads:
        load.start()
    kv_loads = []
    for h in range(HD):
        for part, held in enumerate((wk, wv)):
            kv_loads.append(
                pltpu.make_async_copy(
                    kv_in.at[:, pl.ds(256 * h + 128 * part, 128)], held.at[:, pl.ds(128 * h, 128)], kv_sem.at[part, h]
                )
            )
    for load in kv_loads:
        load.start()
    xq_loads = []
    for part in range(2):
        for n in range(CHIPS):
            parity = 1 - core if part == 0 else core
            row = pl.multiple_of((2 * n + parity) * SH, SH)
            xq_loads.append(
                pltpu.make_async_copy(
                    xq_in.at[pl.ds(row, SH)], xq.at[pl.ds((part * CHIPS + n) * SH, SH)], xq_sem.at[part * CHIPS + n]
                )
            )
    for load in xq_loads:
        load.start()
    cache_load = pltpu.make_async_copy(cache_in, cache.at[core], load_sem.at[0])
    cache_load.start()

    owner_row = jnp.broadcast_to(owner_ref[...].astype(F32).reshape(1, TOK), (LAT - KL - RD, TOK))
    owner_row = jnp.where(iota((LAT - KL - RD, TOK), 0) == 0, owner_row, 0.0)
    lat[c] = jnp.concatenate([lat_ref[...].astype(F32), owner_row], axis=0).T.astype(BF16)

    pl.semaphore_wait(barrier, NCTX - 1 + 1 + CHIPS - 1 + 1)

    half = pl.ds(pl.multiple_of(core * 128, 128), 128)
    other_half = pl.ds(pl.multiple_of((1 - core) * 128, 128), 128)
    quarters = [pl.ds(pl.multiple_of(core * 128 + 64 * n, 64), 64) for n in range(2)]
    handoff = pl.ds(pl.multiple_of(t * SH, SH), SH)

    def y_copy(block, target):
        return remote(
            lat.at[block, half], lat.at[block, half], lat_s.at[target], lat_r.at[block], {"ctx": 4 * x_lo + target, "tp": t}
        )

    def over_copy(block, n):
        return remote(
            lat.at[block, quarters[n]],
            lat.at[block, quarters[n]],
            over_s.at[n, block],
            over_r.at[n, block],
            {"ctx": 4 + y, "tp": (t, across)[n]},
        )

    def ext_copy(source, target):
        return remote(
            lat.at[c, handoff], ext.at[core, source], ext_s.at[target], ext_r.at[source], {"ctx": target, "tp": t}
        )

    def ext_relay(whose):
        return remote(ext.at[whose], ext.at[whose], ext_s.at[NCTX], ext_r.at[NCTX], sibling)

    def cache_relay(whose):
        return remote(cache.at[whose], cache.at[whose], cache_s, cache_r, sibling)

    def relay_copy(source):
        return remote(lat.at[source, half], lat.at[source, half], rel_s.at[source], rel_r.at[source], sibling)

    def relay_arrival(source):
        return remote(
            lat.at[source, other_half], lat.at[source, other_half], rel_s.at[source], rel_r.at[source], sibling
        )

    @pl.when(x_lo == 0)
    def _():
        over_copy(c, 0).start()
        over_copy(c, 1).start()

    for d in (1, 3, 2):
        target = (y + d) % 4

        @pl.when((x_lo == 0) | (target > y))
        def _(target=target):
            y_copy(c, target).start()

    def send_handoff(n, carry):
        @pl.when(n != c)
        def _():
            ext_copy(c, n).start()

        return carry

    ext[core, c] = lat[c, handoff]
    cache_load.wait()
    cache_relay(core).start()

    step_query = sq_ref[...]
    nopes, ropes = [], []
    for n in range(2):
        wq_loads[n].wait()
        up = dot(step_query, wq[n]).astype(BF16).astype(F32)
        for m in range(2):
            for nope, rope in split_pair(up[:, 384 * m : 384 * (m + 1)]):
                nopes.append(nope)
                ropes.append(rope)
    for load in kv_loads:
        load.wait()
    absorbed = jnp.concatenate(
        [dot_t(nopes[h].astype(BF16), wk[:, 128 * h : 128 * (h + 1)]) for h in range(HD)], axis=0
    )
    keys[chip, :, :KL] = absorbed.astype(BF16)
    keys[chip, :, KL:] = jnp.concatenate(ropes, axis=0).astype(BF16)

    def key_across(whose):
        return remote(keys.at[whose], keys.at[whose], key_s.at[0], key_r.at[whose], {"ctx": c, "tp": across})

    def key_copy(whose, d, sem):
        target = {"ctx": c, "tp": 8 * x_hi + 2 * ((z + d) % 4) + core}
        return remote(keys.at[whose], keys.at[whose], key_s.at[sem], key_r.at[whose], target)

    key_across(chip).start()
    for d in (1, 3, 2):
        key_copy(chip, d, d).start()
    lax.fori_loop(0, NCTX, send_handoff, 0)

    wo_loads = [
        pltpu.make_async_copy(wo_in.at[:, pl.ds(CW * n, CW)], wo.at[n], wo_sem.at[n]) for n in range(NCH)
    ]
    for load in wo_loads:
        load.start()

    def hand_on(d):
        @pl.when(x_lo == 0)
        def _():
            block = (y + d) % 4
            y_copy(block, y).wait_recv()
            over_copy(block, 0).start()
            over_copy(block, 1).start()

            @pl.when(block < c)
            def _():
                relay_copy(block).start()

    hand_on(1)

    for load in xq_loads:
        load.wait()
    for n in range(2):
        up = dot(xq[...], wq[n])
        for m in range(2):
            for e, (nope, rope) in enumerate(split_pair(up[:, 384 * m : 384 * (m + 1)])):
                q[4 * n + 2 * m + e, :128] = nope.T.astype(BF16)
                q[4 * n + 2 * m + e, 128:] = rope.T.astype(BF16)

    hand_on(3)
    key_across(opposite).wait_recv()
    for d in (1, 3, 2):
        key_copy(opposite, d, 3 + d).start()
    wv_t[...] = wv[...].T
    hand_on(2)

    column = iota((TOK, TOK), 1)
    parity = jnp.where(column < 128, 1 - core, core)
    position = ((column % 128) // SH) * (2 * SH) + parity * SH + column % SH
    visible = iota((TOK, TOK), 0) <= position

    def fold(block, first):
        latents = lat[block, :, :KL]
        rope = lat[block, :, KL:]
        key = dot(latents, wk[...]).astype(BF16)
        value = dot(wv_t[...], latents.T).astype(BF16)

        def score(h):
            return dot(jnp.concatenate([key[:, 128 * h : 128 * (h + 1)], rope], axis=1), q[h])

        def weigh(h, weights, shrink):
            added = dot(value[128 * h : 128 * (h + 1)], weights)
            if not first:
                added = added + (run_acc[h].reshape(VD // 8, 8, TOK) * shrink[None]).reshape(VD, TOK)
            run_acc[h] = added

        scores = {h: score(h) for h in range(2)}
        late = None
        for h in range(HD):
            if h + 2 < HD:
                scores[h + 2] = score(h + 2)
            if late is not None:
                weigh(*late)
            here = scores.pop(h)
            if first:
                here = jnp.where(visible, here, NEGATIVE)
            here = here.reshape(TOK // 8, 8, TOK)
            top = jnp.max(jnp.max(here, axis=0), axis=0, keepdims=True)
            shrink = None
            if first:
                top = jnp.broadcast_to(top, (8, TOK))
            else:
                old = run_max[h]
                top = jnp.maximum(old, top)
                shrink = jnp.exp2((old - top) * EXP_SCALE)
            raised = jnp.exp2((here - top[None]) * EXP_SCALE)
            total = jnp.sum(raised, axis=0)
            run_max[h] = top
            run_sum[h] = total if first else run_sum[h] * shrink + total
            late = (h, raised.reshape(TOK, TOK).astype(BF16), shrink)
        weigh(*late)

    fold(c, True)

    def forward(block):
        @pl.when(block >= 4)
        def _():
            y_copy(block, y).wait_recv()

        @pl.when(block < 4)
        def _():
            over_copy(block, 0).wait_recv()
            over_copy(block, 1).wait_recv()

        relay_copy(block).start()

    def relay_handoff():
        def one(n, carry):
            @pl.when(n != c)
            def _():
                ext_copy(n, c).wait_recv()

            return carry

        lax.fori_loop(0, NCTX, one, 0)
        ext_relay(core).start()

    def decode():
        for side in range(2):
            for d in range(1, 4):
                whose = 4 * (x_hi if side == 0 else 1 - x_hi) + (z + d) % 4
                key_copy(whose, d, d).wait_recv()
        ext_relay(1 - core).wait_recv()
        cache_relay(1 - core).wait_recv()
        extra = ext[...].reshape(2 * NCTX * SH, LAT)
        cached = cache[...].reshape(2 * ROWB * CPOS, KL + RD)
        shape = (ROWB, 512)
        column = iota(shape, 1)
        length = jnp.zeros(shape, jnp.int32)
        for b in range(ROWB):
            length = jnp.where(column % 256 // CPOS == b, len_ref[b], length)
        place = (2 * chip + column // 256) * CPOS + column % CPOS
        in_cache = (column % 256 // CPOS == iota(shape, 0)) & (place < length)
        pick = jnp.where(iota((ROWB, 128), 1) == RD, 1.0, 0.0).astype(BF16)
        owner = dot_t(pick, extra[:, KL:])
        named = owner == (ROWB * c + iota((ROWB, 256), 0)).astype(F32)
        bias = jnp.concatenate(
            [jnp.where(in_cache, 0.0, NEGATIVE), jnp.where(named, 0.0, NEGATIVE)], axis=1
        ).astype(F32)
        lane = iota((64, 128), 1)
        sub = iota((64, 128), 0)

        def chunk(g):
            query = keys[2 * g : 2 * g + 2].reshape(128, LAT)
            scores = jnp.concatenate(
                [
                    dot_t(query[:, :KL], cached[:, :KL]) + dot_t(query[:, KL : KL + RD], cached[:, KL:]),
                    dot_t(query, extra),
                ],
                axis=1,
            )
            scores = (scores.reshape(16, ROWB, 768) * EXP_SCALE + bias[None]).reshape(128, 768)
            top = jnp.max(scores, axis=1, keepdims=True)
            raised = jnp.exp2(scores - top)
            total = jnp.sum(raised, axis=1, keepdims=True)
            weights = raised.astype(BF16)
            mixed = dot(weights[:, :512], cached[:, :KL]) + dot(weights[:, 512:], extra[:, :KL])
            acc_send[2 * g : 2 * g + 2] = mixed.astype(BF16).reshape(2, 64, KL)
            for n in range(2):
                rows = slice(64 * n, 64 * (n + 1))
                packed = jnp.where(lane == sub, top[rows], 0.0) + jnp.where(lane == sub + 64, total[rows], 0.0)
                ml_send[2 * g + n] = jnp.broadcast_to(jnp.sum(packed, axis=0, keepdims=True), (8, 128))

        for g in range(4):
            chunk(g)

        def send(d, carry):
            target = (chip + d) % CHIPS
            acc_copy(target).start()
            ml_copy(target).start()
            return carry

        lax.fori_loop(1, CHIPS, send, 0)
        acc_recv[chip] = acc_send[chip]
        ml_recv[chip] = ml_send[chip]

    def acc_copy(target):
        return remote(
            acc_send.at[target],
            acc_recv.at[chip],
            acc_s.at[target],
            acc_r.at[chip],
            {"ctx": c, "tp": 2 * target + core},
        )

    def ml_copy(target):
        return remote(
            ml_send.at[target], ml_recv.at[chip], ml_s.at[target], ml_r.at[chip], {"ctx": c, "tp": 2 * target + core}
        )

    def acc_arrival(source):
        return remote(acc_send.at[source], acc_recv.at[source], acc_s.at[source], acc_r.at[source], sibling)

    def ml_arrival(source):
        return remote(ml_send.at[source], ml_recv.at[source], ml_s.at[source], ml_r.at[source], sibling)

    def block_at(n):
        m = n - y - 1
        other_ring = (y + m + (m // 2) * (1 - 2 * (m % 2)) + 8) % 4
        return jnp.where((x_lo == 0) | (n <= y), c - n, other_ring)

    @pl.when(x_lo == 1)
    def _():
        forward(block_at(1))

    def turn(n, carry):
        @pl.when((n < c) & (x_lo == 1))
        def _():
            forward(block_at(n + 1))

        @pl.when(n <= c)
        def _():
            block = block_at(n)
            relay_arrival(block).wait_recv()
            fold(block, False)

        @pl.when(n == 4)
        def _():
            relay_handoff()

        @pl.when(n == 5)
        def _():
            decode()

        return carry

    lax.fori_loop(1, NCTX, turn, 0)

    for h in range(HD):
        total = jnp.sum(run_sum[h], axis=0, keepdims=True)
        head_out[:, 128 * h : 128 * (h + 1)] = (run_acc[h] / total).T.astype(BF16)

    def pair_copy(n):
        return remote(pair_send.at[n], pair_recv.at[n], pair_s.at[n], pair_r.at[n], sibling)

    here_rows = pl.ds(pl.multiple_of(x_hi * 64, 64), 64)
    there_rows = pl.ds(pl.multiple_of(64 - x_hi * 64, 64), 64)

    def row_block(index, count=SH):
        return pl.ds(pl.multiple_of(index * count, count), count)

    def z_device(other):
        return {"ctx": c, "tp": 8 * x_hi + 2 * other + core}

    def x_copy(n):
        return remote(stage.at[n, there_rows], x_recv.at[n], x_s.at[n], x_r.at[n], {"ctx": c, "tp": across})

    def z_copy(n, other):
        return remote(x_sum.at[n, row_block(other)], z_recv.at[n, z], z_s.at[n, other], z_r.at[n, z], z_device(other))

    def z_arrival(n, other):
        return remote(z_recv.at[n, other], z_recv.at[n, other], z_s.at[n, other], z_r.at[n, other], sibling)

    def first_z_copy(n, other):
        return remote(
            stage.at[n, row_block(other, 2 * SH)], zz_recv.at[n, z], z_s.at[n, other], z_r.at[n, z], z_device(other)
        )

    def first_z_arrival(n, other):
        return remote(zz_recv.at[n, other], zz_recv.at[n, other], z_s.at[n, other], z_r.at[n, other], sibling)

    def last_x_copy(n):
        return remote(
            x_sum.at[n, row_block(1 - x_hi)], x_recv.at[n, :SH], x_s.at[n], x_r.at[n], {"ctx": c, "tp": across}
        )

    def project(n):
        wo_load = pltpu.make_async_copy(wo_in.at[:, pl.ds(CW * n, CW)], wo.at[n], wo_sem.at[n])
        wo_load.wait()
        for m in range(CW // 256):
            columns = slice(256 * m, 256 * (m + 1))
            term = dot(head_out[...], wo[n, :, columns])
            pair_send[n, :, columns] = term[:128].astype(BF16)
            own[n, :, columns] = term[128:].astype(BF16)
        pair_copy(n).start()

    def add_core(n):
        pair_copy(n).wait_recv()
        both = (own[n].astype(F32) + pair_recv[n].astype(F32)).astype(BF16)

        @pl.when(n % 2 == 0)
        def _():
            stage[n] = both
            x_copy(n).start()

        @pl.when(n % 2 == 1)
        def _():
            for other in range(4):
                for side in range(2):
                    to, of = (2 * other + side) * SH, (4 * side + other) * SH
                    stage[n, to : to + SH] = both[of : of + SH]
            for d in (1, 3, 2):
                first_z_copy(n, (z + d) % 4).start()

    def add_chips(n):
        @pl.when(n % 2 == 0)
        def _():
            x_copy(n).wait_recv()
            x_sum[n] = (stage[n, here_rows].astype(F32) + x_recv[n].astype(F32)).astype(BF16)
            for d in (1, 3, 2):
                z_copy(n, (z + d) % 4).start()
            z_recv[n, z] = x_sum[n, row_block(z)]

        @pl.when(n % 2 == 1)
        def _():
            summed = stage[n, row_block(z, 2 * SH)].astype(F32)
            for d in (1, 3, 2):
                other = (z + d) % 4
                first_z_arrival(n, other).wait_recv()
                summed = summed + zz_recv[n, other].astype(F32)
            x_sum[n, : 2 * SH] = summed.astype(BF16)
            last_x_copy(n).start()

    def column_turn(n, carry):
        @pl.when(n < NCH)
        def _():
            project(n)

        @pl.when((n >= 1) & (n < NCH + 1))
        def _():
            add_core(n - 1)

        @pl.when(n >= 3)
        def _():
            add_chips(n - 3)

        return carry

    lax.fori_loop(0, NCH + 3, column_turn, 0)

    def merge_arrivals(d, carry):
        source = (chip + d) % CHIPS
        acc_arrival(source).wait_recv()
        ml_arrival(source).wait_recv()
        return carry

    lax.fori_loop(1, CHIPS, merge_arrivals, 0)
    lane = iota((64, 128), 1)
    sub = iota((64, 128), 0)
    tops, totals = [], []
    for s in range(CHIPS):
        packed = jnp.broadcast_to(ml_recv[s, 0:1, :], (64, 128))
        tops.append(jnp.sum(jnp.where(lane == sub, packed, 0.0), axis=1, keepdims=True))
        totals.append(jnp.sum(jnp.where(lane == sub + 64, packed, 0.0), axis=1, keepdims=True))
    top = tops[0]
    for s in range(1, CHIPS):
        top = jnp.maximum(top, tops[s])
    total = jnp.zeros((64, 1), F32)
    summed = jnp.zeros((64, KL), F32)
    for s in range(CHIPS):
        weight = jnp.exp2(tops[s] - top)
        total = total + totals[s] * weight
        summed = summed + acc_recv[s].astype(F32) * weight
    mixed = summed / total
    for h in range(HD):
        step_ref[:, 128 * h : 128 * (h + 1)] = dot(
            mixed[ROWB * h : ROWB * (h + 1)].astype(BF16), wv[:, 128 * h : 128 * (h + 1)]
        )

    for n in range(NCH):
        if n % 2 == 0:
            for d in range(1, 4):
                z_arrival(n, (z + d) % 4).wait_recv()
            summed = z_recv[n, 0].astype(F32)
            for other in range(1, 4):
                summed = summed + z_recv[n, other].astype(F32)
        else:
            last_x_copy(n).wait_recv()
            summed = x_sum[n, row_block(x_hi)].astype(F32) + x_recv[n, :SH].astype(F32)
        out_ref[:, CW * n : CW * (n + 1)] = summed

    def drain_ctx(n, carry):
        @pl.when(n < c)
        def _():
            relay_copy(n).wait_send()

        @pl.when(n != c)
        def _():
            ext_copy(c, n).wait_send()

        @pl.when(n != chip)
        def _():
            acc_copy(n).wait_send()
            ml_copy(n).wait_send()

        return carry

    lax.fori_loop(0, NCTX, drain_ctx, 0)

    @pl.when(x_lo == 0)
    def _():
        for block in range(4):
            over_copy(block, 0).wait_send()
            over_copy(block, 1).wait_send()

    for d in (1, 3, 2):
        target = (y + d) % 4

        @pl.when((x_lo == 0) | (target > y))
        def _(target=target):
            y_copy(c, target).wait_send()

    key_across(chip).wait_send()
    for d in (1, 3, 2):
        key_copy(chip, d, d).wait_send()
        key_copy(opposite, d, 3 + d).wait_send()
    ext_relay(core).wait_send()
    cache_relay(core).wait_send()

    def drain_columns(n, carry):
        pair_copy(n).wait_send()

        @pl.when(n % 2 == 0)
        def _():
            x_copy(n).wait_send()
            for d in range(1, 4):
                z_copy(n, (z + d) % 4).wait_send()

        @pl.when(n % 2 == 1)
        def _():
            last_x_copy(n).wait_send()
            for d in range(1, 4):
                first_z_copy(n, (z + d) % 4).wait_send()

        return carry

    lax.fori_loop(0, NCH, drain_columns, 0)


def place(span_in, step_in, span_out, step_out):
    span_out[...] = span_in[...]
    step_out[...] = step_in[...]


def body(
    span_query,
    span_latent,
    query_up,
    key_value_up,
    out_weight,
    owner_rows,
    step_query,
    latent_cache,
    cache_lengths,
):
    dma = pltpu.SemaphoreType.DMA
    vmem = pltpu.VMEM
    anywhere = pl.BlockSpec(memory_space=pl.ANY)
    in_vmem = pl.BlockSpec(memory_space=pltpu.VMEM)
    out_shape = (
        jax.ShapeDtypeStruct((SH, D), F32),
        jax.ShapeDtypeStruct((ROWB, HD * VD), F32),
    )
    results = pl.pallas_call(
        kernel,
        out_shape=out_shape,
        in_specs=[in_vmem] * 2 + [anywhere] * 4 + [in_vmem, anywhere, pl.BlockSpec(memory_space=pltpu.SMEM)],
        out_specs=(in_vmem, in_vmem),
        scratch_shapes=[
            vmem((NCTX, TOK, LAT), BF16),
            vmem((2, NCTX, SH, LAT), BF16),
            vmem((TOK, QL), BF16),
            vmem((2, QL, 768), BF16),
            vmem((KL, HD * NOPE), BF16),
            vmem((KL, HD * VD), BF16),
            vmem((HD * VD, KL), BF16),
            vmem((NCH, HD * VD, CW), BF16),
            vmem((2, ROWB * CPOS, KL + RD), BF16),
            vmem((HD, TOK, 256), BF16),
            vmem((HD, 8, TOK), F32),
            vmem((HD, 8, TOK), F32),
            vmem((HD, VD, TOK), F32),
            vmem((TOK, HD * VD), BF16),
            vmem((CHIPS, 64, LAT), BF16),
            vmem((CHIPS, 64, KL), BF16),
            vmem((CHIPS, 64, KL), BF16),
            vmem((CHIPS, 8, 128), F32),
            vmem((CHIPS, 8, 128), F32),
            vmem((NCH, 128, CW), BF16),
            vmem((NCH, 128, CW), BF16),
            vmem((NCH, 128, CW), BF16),
            vmem((NCH, 128, CW), BF16),
            vmem((NCH, 64, CW), BF16),
            vmem((NCH, 64, CW), BF16),
            vmem((NCH, 4, SH, CW), BF16),
            vmem((NCH, 4, 2 * SH, CW), BF16),
            dma((1,)),
            dma((2, HD)),
            dma((2,)),
            dma((NCH,)),
            dma((2 * CHIPS,)),
            dma((4,)),
            dma((NCTX,)),
            dma((2, 4)),
            dma((2, 4)),
            dma((NCTX,)),
            dma((NCTX,)),
            dma((NCTX + 1,)),
            dma((NCTX + 1,)),
            dma,
            dma,
            dma((CHIPS,)),
            dma((CHIPS,)),
            dma((CHIPS,)),
            dma((CHIPS,)),
            dma((CHIPS,)),
            dma((CHIPS,)),
            dma((NCH,)),
            dma((NCH,)),
            dma((NCH,)),
            dma((NCH,)),
            dma((NCH, 4)),
            dma((NCH, 4)),
        ],
        compiler_params=pltpu.CompilerParams(
            collective_id=0, has_side_effects=True, vmem_limit_bytes=60 * 1024 * 1024
        ),
        name="attention",
    )(
        span_latent.T,
        owner_rows,
        span_query,
        query_up,
        key_value_up,
        out_weight,
        step_query,
        latent_cache.reshape(ROWB * CPOS, KL + RD),
        cache_lengths,
    )
    return pl.pallas_call(
        place,
        out_shape=out_shape,
        in_specs=[in_vmem] * 2,
        out_specs=(in_vmem, in_vmem),
        name="place",
    )(*results)


def solution(mesh):
    in_specs = (
        P("ctx", None),
        P("ctx", None),
        P(None, "tp"),
        P(None, "tp"),
        P("tp", None),
        P("ctx"),
        P("ctx", None),
        P("ctx", "tp", None),
        P("ctx"),
    )
    out_specs = (P(("ctx", "tp"), None), P("ctx", "tp"))
    return jax.shard_map(body, mesh=mesh, in_specs=in_specs, out_specs=out_specs, check_vma=False)
```

```python
import math

import jax
import jax.numpy as jnp
from jax import lax
from jax.experimental import pallas as pl
from jax.experimental.pallas import tpu as pltpu
from jax.sharding import PartitionSpec as P

KL = 512
RD = 64
NOPE = 128
VD = 128
HD = 8
TOK = 256
LAT = 640
ROWB = 8
CPOS = 32
QL = 1536
D = 7168
NCTX = 8
NTP = 16
CHIPS = 8
NCH = 7
CW = D // NCH
SH = 16
NEGATIVE = -1e30
EXP_SCALE = (NOPE + RD) ** -0.5 * math.log2(math.e)
MESH = pl.DeviceIdType.MESH
F32 = jnp.float32
BF16 = jnp.bfloat16


def dot(a, b):
    return jnp.dot(a, b, preferred_element_type=F32)


def dot_t(a, b):
    return lax.dot_general(a, b, (((1,), (1,)), ((), ())), preferred_element_type=F32)


def iota(shape, dim):
    return lax.broadcasted_iota(jnp.int32, shape, dim)


def split_pair(y):
    rows = y.shape[0]
    low = iota((rows, 128), 1) < 64
    first, middle, last = y[:, :128], y[:, 128:256], y[:, 256:384]
    middle_turned = pltpu.roll(middle, 64, 1)
    last_turned = pltpu.roll(last, 64, 1)
    zero = jnp.zeros_like(first)
    return (
        (first, jnp.where(low, middle, zero)),
        (jnp.where(low, middle_turned, last_turned), jnp.where(low, last_turned, zero)),
    )


def kernel(
    lat_ref, owner_ref, xq_in, wq_in, kv_in, wo_in, sq_ref, cache_in, len_ref,
    out_ref, step_ref,
    lat, ext, xq, wq, wk, wv, wv_t, wo, cache, q, run_max, run_sum, run_acc, head_out,
    keys, acc_send, acc_recv, ml_send, ml_recv,
    pair_send, own, pair_recv, stage, x_recv, x_sum, z_recv, zz_recv,
    load_sem, kv_sem, wq_sem, wo_sem, xq_sem,
    lat_s, lat_r, over_s, over_r, rel_s, rel_r, ext_s, ext_r, hand_s, hand_r, cache_s, cache_r, key_s, key_r,
    acc_s, acc_r, ml_s, ml_r, pair_s, pair_r, x_s, x_r, z_s, z_r,
):
    c = lax.axis_index("ctx")
    t = lax.axis_index("tp")
    core = t % 2
    chip = t // 2
    sibling = {"ctx": c, "tp": t + 1 - 2 * core}
    across = (t + CHIPS) % NTP
    opposite = (chip + 4) % CHIPS
    x_hi = chip // 4
    z = chip % 4
    x_lo = c // 4
    y = c % 4

    def remote(src, dst, send, recv, device):
        return pltpu.make_async_remote_copy(
            src_ref=src, dst_ref=dst, send_sem=send, recv_sem=recv, device_id=device, device_id_type=MESH
        )

    wq_loads = [
        pltpu.make_async_copy(wq_in.at[:, pl.ds(768 * n, 768)], wq.at[n], wq_sem.at[n]) for n in range(2)
    ]
    for load in wq_loads:
        load.start()

    barrier = pltpu.get_barrier_semaphore()
    for d in range(1, NCTX):
        pl.semaphore_signal(barrier, inc=1, device_id={"ctx": (c + d) % NCTX, "tp": t}, device_id_type=MESH)
    pl.semaphore_signal(barrier, inc=1, device_id={"ctx": (c + 4) % NCTX, "tp": across}, device_id_type=MESH)
    for d in range(1, CHIPS):
        pl.semaphore_signal(barrier, inc=1, device_id={"ctx": c, "tp": (t + 2 * d) % NTP}, device_id_type=MESH)
    pl.semaphore_signal(barrier, inc=1, device_id=sibling, device_id_type=MESH)

    owner_row = jnp.broadcast_to(owner_ref[...].astype(F32).reshape(1, TOK), (LAT - KL - RD, TOK))
    owner_row = jnp.where(iota((LAT - KL - RD, TOK), 0) == 0, owner_row, 0.0)
    lat[c] = jnp.concatenate([lat_ref[...].astype(F32), owner_row], axis=0).T.astype(BF16)

    pl.semaphore_wait(barrier, NCTX - 1 + 1 + CHIPS - 1 + 1)

    half = pl.ds(pl.multiple_of(core * 128, 128), 128)
    other_half = pl.ds(pl.multiple_of((1 - core) * 128, 128), 128)
    quarters = [pl.ds(pl.multiple_of(core * 128 + 64 * n, 64), 64) for n in range(2)]
    handoff = pl.ds(pl.multiple_of(t * SH, SH), SH)

    def y_copy(block, target):
        return remote(
            lat.at[block, half], lat.at[block, half], lat_s.at[target], lat_r.at[block], {"ctx": 4 * x_lo + target, "tp": t}
        )

    def over_copy(block, n):
        return remote(
            lat.at[block, quarters[n]],
            lat.at[block, quarters[n]],
            over_s.at[n, block],
            over_r.at[n, block],
            {"ctx": 4 + y, "tp": (t, across)[n]},
        )

    def ext_copy(source, target):
        return remote(
            lat.at[c, handoff], ext.at[core, source], ext_s.at[target], ext_r.at[source], {"ctx": target, "tp": t}
        )

    def whole(source):
        return ((x_lo == 0) & (source < 4)) | ((x_lo == 1) & (source <= c))

    def ext_relay(source, whose):
        return remote(
            ext.at[whose, source], ext.at[whose, source], hand_s.at[source], hand_r.at[source], sibling
        )

    def cache_relay(whose):
        return remote(cache.at[whose], cache.at[whose], cache_s, cache_r, sibling)

    def relay_copy(source):
        return remote(lat.at[source, half], lat.at[source, half], rel_s.at[source], rel_r.at[source], sibling)

    def relay_arrival(source):
        return remote(
            lat.at[source, other_half], lat.at[source, other_half], rel_s.at[source], rel_r.at[source], sibling
        )

    @pl.when(x_lo == 0)
    def _():
        over_copy(c, 0).start()
        over_copy(c, 1).start()

    for d in (1, 3, 2):
        target = (y + d) % 4

        @pl.when((x_lo == 0) | (target > y))
        def _(target=target):
            y_copy(c, target).start()

    kv_loads = []
    for h in range(HD):
        for part, held in enumerate((wk, wv)):
            kv_loads.append(
                pltpu.make_async_copy(
                    kv_in.at[:, pl.ds(256 * h + 128 * part, 128)], held.at[:, pl.ds(128 * h, 128)], kv_sem.at[part, h]
                )
            )
    for load in kv_loads:
        load.start()
    xq_loads = []
    for part in range(2):
        for n in range(CHIPS):
            parity = 1 - core if part == 0 else core
            row = pl.multiple_of((2 * n + parity) * SH, SH)
            xq_loads.append(
                pltpu.make_async_copy(
                    xq_in.at[pl.ds(row, SH)], xq.at[pl.ds((part * CHIPS + n) * SH, SH)], xq_sem.at[part * CHIPS + n]
                )
            )
    for load in xq_loads:
        load.start()
    cache_load = pltpu.make_async_copy(cache_in, cache.at[core], load_sem.at[0])
    cache_load.start()


    def send_handoff(n, carry):
        @pl.when((x_lo == 1) & (n < c))
        def _():
            ext_copy(c, n).start()

        return carry

    cache_load.wait()
    cache_relay(core).start()

    for load in xq_loads:
        load.wait()
    xq[TOK:] = jnp.concatenate([sq_ref[...].astype(F32), jnp.zeros((ROWB, QL), F32)], axis=0).astype(BF16)
    nopes, ropes = [], []
    for n in range(2):
        wq_loads[n].wait()
        up = dot(xq[...], wq[n])
        for m in range(2):
            for e, (nope, rope) in enumerate(split_pair(up[:, 384 * m : 384 * (m + 1)])):
                q[4 * n + 2 * m + e, :128] = nope[:TOK].T.astype(BF16)
                q[4 * n + 2 * m + e, 128:] = rope[:TOK].T.astype(BF16)
                nopes.append(nope[TOK : TOK + ROWB])
                ropes.append(rope[TOK : TOK + ROWB])

    for load in kv_loads:
        load.wait()
    absorbed = jnp.concatenate(
        [dot_t(nopes[h].astype(BF16), wk[:, 128 * h : 128 * (h + 1)]) for h in range(HD)], axis=0
    )
    keys[chip, :, :KL] = absorbed.astype(BF16)
    keys[chip, :, KL:] = jnp.concatenate(ropes, axis=0).astype(BF16)

    def key_across(whose):
        return remote(keys.at[whose], keys.at[whose], key_s.at[0], key_r.at[whose], {"ctx": c, "tp": across})

    def key_copy(whose, d, sem):
        target = {"ctx": c, "tp": 8 * x_hi + 2 * ((z + d) % 4) + core}
        return remote(keys.at[whose], keys.at[whose], key_s.at[sem], key_r.at[whose], target)

    key_across(chip).start()
    for d in (1, 3, 2):
        key_copy(chip, d, d).start()
    lax.fori_loop(0, NCTX, send_handoff, 0)

    wo_loads = [
        pltpu.make_async_copy(wo_in.at[:, pl.ds(CW * n, CW)], wo.at[n], wo_sem.at[n]) for n in range(NCH)
    ]
    for load in wo_loads:
        load.start()

    def hand_on(d):
        @pl.when(x_lo == 0)
        def _():
            block = (y + d) % 4
            y_copy(block, y).wait_recv()
            over_copy(block, 0).start()
            over_copy(block, 1).start()

            relay_copy(block).start()

    hand_on(1)

    wv_t[...] = wv[...].T
    hand_on(3)

    column = iota((TOK, TOK), 1)
    parity = jnp.where(column < 128, 1 - core, core)
    position = ((column % 128) // SH) * (2 * SH) + parity * SH + column % SH
    visible = iota((TOK, TOK), 0) <= position

    def fold(block, first):
        latents = lat[block, :, :KL]
        rope = lat[block, :, KL:]
        key = dot(latents, wk[...]).astype(BF16)
        value = dot(wv_t[...], latents.T).astype(BF16)

        def score(h):
            return dot(jnp.concatenate([key[:, 128 * h : 128 * (h + 1)], rope], axis=1), q[h])

        def weigh(h, weights, shrink):
            added = dot(value[128 * h : 128 * (h + 1)], weights)
            if not first:
                added = added + (run_acc[h].reshape(VD // 8, 8, TOK) * shrink[None]).reshape(VD, TOK)
            run_acc[h] = added

        scores = {h: score(h) for h in range(2)}
        late = None
        for h in range(HD):
            if h + 2 < HD:
                scores[h + 2] = score(h + 2)
            if late is not None:
                weigh(*late)
            here = scores.pop(h)
            if first:
                here = jnp.where(visible, here, NEGATIVE)
            here = here.reshape(TOK // 8, 8, TOK)
            top = jnp.max(jnp.max(here, axis=0), axis=0, keepdims=True)
            shrink = None
            if first:
                top = jnp.broadcast_to(top, (8, TOK))
            else:
                old = run_max[h]
                top = jnp.maximum(old, top)
                shrink = jnp.exp2((old - top) * EXP_SCALE)
            raised = jnp.exp2((here - top[None]) * EXP_SCALE)
            total = jnp.sum(raised, axis=0)
            run_max[h] = top
            run_sum[h] = total if first else run_sum[h] * shrink + total
            late = (h, raised.reshape(TOK, TOK).astype(BF16), shrink)
        weigh(*late)

    def forward(block):
        @pl.when(block >= 4)
        def _():
            y_copy(block, y).wait_recv()

        @pl.when(block < 4)
        def _():
            over_copy(block, 0).wait_recv()
            over_copy(block, 1).wait_recv()

        relay_copy(block).start()

    def block_at(n):
        m = n - y - 1
        other_ring = (y + m + (m // 2) * (1 - 2 * (m % 2)) + 8) % 4
        return jnp.where((x_lo == 0) | (n <= y), c - n, other_ring)

    @pl.when(x_lo == 1)
    def _():
        forward(block_at(1))

    fold(c, True)
    hand_on(2)
    key_across(opposite).wait_recv()
    for d in (1, 3, 2):
        key_copy(opposite, d, 3 + d).start()

    def relay_handoff():
        def one(n, carry):
            @pl.when(jnp.logical_not(whole(n)))
            def _():
                ext_copy(n, c).wait_recv()
                ext_relay(n, core).start()

            return carry

        lax.fori_loop(0, NCTX, one, 0)

    def decode():
        for side in range(2):
            for d in range(1, 4):
                whose = 4 * (x_hi if side == 0 else 1 - x_hi) + (z + d) % 4
                key_copy(whose, d, d).wait_recv()
        def gather(n, carry):
            @pl.when((x_lo == 0) & (n > c) & (n < 4))
            def _():
                relay_arrival(n).wait_recv()

            @pl.when(whole(n))
            def _():
                for whose in range(2):
                    ext[whose, n] = lat[n, pl.ds(pl.multiple_of((2 * chip + whose) * SH, SH), SH)]

            @pl.when(jnp.logical_not(whole(n)))
            def _():
                ext_relay(n, 1 - core).wait_recv()

            return carry

        lax.fori_loop(0, NCTX, gather, 0)
        cache_relay(1 - core).wait_recv()
        extra = ext[...].reshape(2 * NCTX * SH, LAT)
        cached = cache[...].reshape(2 * ROWB * CPOS, KL + RD)
        shape = (ROWB, 512)
        column = iota(shape, 1)
        length = jnp.zeros(shape, jnp.int32)
        for b in range(ROWB):
            length = jnp.where(column % 256 // CPOS == b, len_ref[b], length)
        place = (2 * chip + column // 256) * CPOS + column % CPOS
        in_cache = (column % 256 // CPOS == iota(shape, 0)) & (place < length)
        pick = jnp.where(iota((ROWB, 128), 1) == RD, 1.0, 0.0).astype(BF16)
        owner = dot_t(pick, extra[:, KL:])
        named = owner == (ROWB * c + iota((ROWB, 256), 0)).astype(F32)
        bias = jnp.concatenate(
            [jnp.where(in_cache, 0.0, NEGATIVE), jnp.where(named, 0.0, NEGATIVE)], axis=1
        ).astype(F32)
        lane = iota((64, 128), 1)
        sub = iota((64, 128), 0)

        def chunk(g):
            query = keys[4 * g : 4 * g + 4].reshape(256, LAT)
            scores = jnp.concatenate(
                [
                    dot_t(query[:, :KL], cached[:, :KL]) + dot_t(query[:, KL : KL + RD], cached[:, KL:]),
                    dot_t(query, extra),
                ],
                axis=1,
            )
            scores = (scores.reshape(32, ROWB, 768) * EXP_SCALE + bias[None]).reshape(256, 768)
            top = jnp.max(scores, axis=1, keepdims=True)
            raised = jnp.exp2(scores - top)
            total = jnp.sum(raised, axis=1, keepdims=True)
            weights = raised.astype(BF16)
            mixed = dot(weights[:, :512], cached[:, :KL]) + dot(weights[:, 512:], extra[:, :KL])
            acc_send[4 * g : 4 * g + 4] = mixed.astype(BF16).reshape(4, 64, KL)
            for n in range(4):
                rows = slice(64 * n, 64 * (n + 1))
                packed = jnp.where(lane == sub, top[rows], 0.0) + jnp.where(lane == sub + 64, total[rows], 0.0)
                ml_send[4 * g + n] = jnp.broadcast_to(jnp.sum(packed, axis=0, keepdims=True), (8, 128))

        for g in range(2):
            chunk(g)

        def send(d, carry):
            target = (chip + d) % CHIPS
            acc_copy(target).start()
            ml_copy(target).start()
            return carry

        lax.fori_loop(1, CHIPS, send, 0)
        acc_recv[chip] = acc_send[chip]
        ml_recv[chip] = ml_send[chip]

    def acc_copy(target):
        return remote(
            acc_send.at[target],
            acc_recv.at[chip],
            acc_s.at[target],
            acc_r.at[chip],
            {"ctx": c, "tp": 2 * target + core},
        )

    def ml_copy(target):
        return remote(
            ml_send.at[target], ml_recv.at[chip], ml_s.at[target], ml_r.at[chip], {"ctx": c, "tp": 2 * target + core}
        )

    def acc_arrival(source):
        return remote(acc_send.at[source], acc_recv.at[source], acc_s.at[source], acc_r.at[source], sibling)

    def ml_arrival(source):
        return remote(ml_send.at[source], ml_recv.at[source], ml_s.at[source], ml_r.at[source], sibling)

    def turn(n, carry):
        @pl.when(n == 3)
        def _():
            relay_handoff()

        @pl.when((n < c) & (x_lo == 1))
        def _():
            forward(block_at(n + 1))

        @pl.when(n <= c)
        def _():
            block = block_at(n)
            relay_arrival(block).wait_recv()

        @pl.when(n == jnp.where(x_lo == 1, c, NCTX - 1))
        def _():
            decode()

        @pl.when(n <= c)
        def _():
            fold(block_at(n), False)

        return carry

    lax.fori_loop(1, NCTX, turn, 0)

    for h in range(HD):
        total = jnp.sum(run_sum[h], axis=0, keepdims=True)
        head_out[:, 128 * h : 128 * (h + 1)] = (run_acc[h] / total).T.astype(BF16)

    def pair_copy(n):
        return remote(pair_send.at[n], pair_recv.at[n], pair_s.at[n], pair_r.at[n], sibling)

    here_rows = pl.ds(pl.multiple_of(x_hi * 64, 64), 64)
    there_rows = pl.ds(pl.multiple_of(64 - x_hi * 64, 64), 64)

    def row_block(index, count=SH):
        return pl.ds(pl.multiple_of(index * count, count), count)

    def z_device(other):
        return {"ctx": c, "tp": 8 * x_hi + 2 * other + core}

    def z_first(n):
        return n % 2 == 1

    def x_copy(n):
        return remote(stage.at[n, there_rows], x_recv.at[n], x_s.at[n], x_r.at[n], {"ctx": c, "tp": across})

    def z_copy(n, other):
        return remote(x_sum.at[n, row_block(other)], z_recv.at[n, z], z_s.at[n, other], z_r.at[n, z], z_device(other))

    def z_arrival(n, other):
        return remote(z_recv.at[n, other], z_recv.at[n, other], z_s.at[n, other], z_r.at[n, other], sibling)

    def first_z_copy(n, other):
        return remote(
            stage.at[n, row_block(other, 2 * SH)], zz_recv.at[n, z], z_s.at[n, other], z_r.at[n, z], z_device(other)
        )

    def first_z_arrival(n, other):
        return remote(zz_recv.at[n, other], zz_recv.at[n, other], z_s.at[n, other], z_r.at[n, other], sibling)

    def last_x_copy(n):
        return remote(
            x_sum.at[n, row_block(1 - x_hi)], x_recv.at[n, :SH], x_s.at[n], x_r.at[n], {"ctx": c, "tp": across}
        )

    def project(n):
        wo_load = pltpu.make_async_copy(wo_in.at[:, pl.ds(CW * n, CW)], wo.at[n], wo_sem.at[n])
        wo_load.wait()
        for m in range(CW // 256):
            columns = slice(256 * m, 256 * (m + 1))
            term = dot(head_out[...], wo[n, :, columns])
            pair_send[n, :, columns] = term[:128].astype(BF16)
            own[n, :, columns] = term[128:].astype(BF16)
        pair_copy(n).start()

    def add_core(n):
        pair_copy(n).wait_recv()
        both = (own[n].astype(F32) + pair_recv[n].astype(F32)).astype(BF16)

        @pl.when(jnp.logical_not(z_first(n)))
        def _():
            stage[n] = both
            x_copy(n).start()

        @pl.when(z_first(n))
        def _():
            for other in range(4):
                for side in range(2):
                    to, of = (2 * other + side) * SH, (4 * side + other) * SH
                    stage[n, to : to + SH] = both[of : of + SH]
            for d in (1, 3, 2):
                first_z_copy(n, (z + d) % 4).start()

    def add_chips(n):
        @pl.when(jnp.logical_not(z_first(n)))
        def _():
            x_copy(n).wait_recv()
            x_sum[n] = (stage[n, here_rows].astype(F32) + x_recv[n].astype(F32)).astype(BF16)
            for d in (1, 3, 2):
                z_copy(n, (z + d) % 4).start()
            z_recv[n, z] = x_sum[n, row_block(z)]

        @pl.when(z_first(n))
        def _():
            summed = stage[n, row_block(z, 2 * SH)].astype(F32)
            for d in (1, 3, 2):
                other = (z + d) % 4
                first_z_arrival(n, other).wait_recv()
                summed = summed + zz_recv[n, other].astype(F32)
            x_sum[n, : 2 * SH] = summed.astype(BF16)
            last_x_copy(n).start()

    def column_turn(n, carry):
        @pl.when(n < NCH)
        def _():
            project(n)

        @pl.when((n >= 1) & (n < NCH + 1))
        def _():
            add_core(n - 1)

        @pl.when(n >= 3)
        def _():
            add_chips(n - 3)

        return carry

    lax.fori_loop(0, NCH + 3, column_turn, 0)

    def merge_arrivals(d, carry):
        source = (chip + d) % CHIPS
        acc_arrival(source).wait_recv()
        ml_arrival(source).wait_recv()
        return carry

    lax.fori_loop(1, CHIPS, merge_arrivals, 0)
    lane = iota((64, 128), 1)
    sub = iota((64, 128), 0)
    tops, totals = [], []
    for s in range(CHIPS):
        packed = jnp.broadcast_to(ml_recv[s, 0:1, :], (64, 128))
        tops.append(jnp.sum(jnp.where(lane == sub, packed, 0.0), axis=1, keepdims=True))
        totals.append(jnp.sum(jnp.where(lane == sub + 64, packed, 0.0), axis=1, keepdims=True))
    top = tops[0]
    for s in range(1, CHIPS):
        top = jnp.maximum(top, tops[s])
    total = jnp.zeros((64, 1), F32)
    summed = jnp.zeros((64, KL), F32)
    for s in range(CHIPS):
        weight = jnp.exp2(tops[s] - top)
        total = total + totals[s] * weight
        summed = summed + acc_recv[s].astype(F32) * weight
    mixed = summed / total
    for h in range(HD):
        step_ref[:, 128 * h : 128 * (h + 1)] = dot(
            mixed[ROWB * h : ROWB * (h + 1)].astype(BF16), wv[:, 128 * h : 128 * (h + 1)]
        )

    def sum_z(n):
        for d in range(1, 4):
            z_arrival(n, (z + d) % 4).wait_recv()
        summed = z_recv[n, 0].astype(F32)
        for other in range(1, 4):
            summed = summed + z_recv[n, other].astype(F32)
        out_ref[:, CW * n : CW * (n + 1)] = summed

    def sum_x(n):
        last_x_copy(n).wait_recv()
        summed = x_sum[n, row_block(x_hi)].astype(F32) + x_recv[n, :SH].astype(F32)
        out_ref[:, CW * n : CW * (n + 1)] = summed

    for n in range(NCH):
        if z_first(n):
            sum_x(n)
        else:
            sum_z(n)

    def drain_ctx(n, carry):
        @pl.when((n != c) & whole(n))
        def _():
            relay_copy(n).wait_send()

        @pl.when((x_lo == 1) & (n < c))
        def _():
            ext_copy(c, n).wait_send()

        @pl.when(jnp.logical_not(whole(n)))
        def _():
            ext_relay(n, core).wait_send()

        @pl.when(n != chip)
        def _():
            acc_copy(n).wait_send()
            ml_copy(n).wait_send()

        return carry

    lax.fori_loop(0, NCTX, drain_ctx, 0)

    @pl.when(x_lo == 0)
    def _():
        for block in range(4):
            over_copy(block, 0).wait_send()
            over_copy(block, 1).wait_send()

    for d in (1, 3, 2):
        target = (y + d) % 4

        @pl.when((x_lo == 0) | (target > y))
        def _(target=target):
            y_copy(c, target).wait_send()

    key_across(chip).wait_send()
    for d in (1, 3, 2):
        key_copy(chip, d, d).wait_send()
        key_copy(opposite, d, 3 + d).wait_send()
    cache_relay(core).wait_send()

    def drain_columns(n, carry):
        pair_copy(n).wait_send()

        @pl.when(jnp.logical_not(z_first(n)))
        def _():
            x_copy(n).wait_send()
            for d in range(1, 4):
                z_copy(n, (z + d) % 4).wait_send()

        @pl.when(z_first(n))
        def _():
            last_x_copy(n).wait_send()
            for d in range(1, 4):
                first_z_copy(n, (z + d) % 4).wait_send()

        return carry

    lax.fori_loop(0, NCH, drain_columns, 0)


def place(span_in, step_in, span_out, step_out):
    span_out[...] = span_in[...]
    step_out[...] = step_in[...]


def body(
    span_query,
    span_latent,
    query_up,
    key_value_up,
    out_weight,
    owner_rows,
    step_query,
    latent_cache,
    cache_lengths,
):
    dma = pltpu.SemaphoreType.DMA
    vmem = pltpu.VMEM
    anywhere = pl.BlockSpec(memory_space=pl.ANY)
    in_vmem = pl.BlockSpec(memory_space=pltpu.VMEM)
    out_shape = (
        jax.ShapeDtypeStruct((SH, D), F32),
        jax.ShapeDtypeStruct((ROWB, HD * VD), F32),
    )
    results = pl.pallas_call(
        kernel,
        out_shape=out_shape,
        in_specs=[in_vmem] * 2 + [anywhere] * 4 + [in_vmem, anywhere, pl.BlockSpec(memory_space=pltpu.SMEM)],
        out_specs=(in_vmem, in_vmem),
        scratch_shapes=[
            vmem((NCTX, TOK, LAT), BF16),
            vmem((2, NCTX, SH, LAT), BF16),
            vmem((TOK + 2 * ROWB, QL), BF16),
            vmem((2, QL, 768), BF16),
            vmem((KL, HD * NOPE), BF16),
            vmem((KL, HD * VD), BF16),
            vmem((HD * VD, KL), BF16),
            vmem((NCH, HD * VD, CW), BF16),
            vmem((2, ROWB * CPOS, KL + RD), BF16),
            vmem((HD, TOK, 256), BF16),
            vmem((HD, 8, TOK), F32),
            vmem((HD, 8, TOK), F32),
            vmem((HD, VD, TOK), F32),
            vmem((TOK, HD * VD), BF16),
            vmem((CHIPS, 64, LAT), BF16),
            vmem((CHIPS, 64, KL), BF16),
            vmem((CHIPS, 64, KL), BF16),
            vmem((CHIPS, 8, 128), F32),
            vmem((CHIPS, 8, 128), F32),
            vmem((NCH, 128, CW), BF16),
            vmem((NCH, 128, CW), BF16),
            vmem((NCH, 128, CW), BF16),
            vmem((NCH, 128, CW), BF16),
            vmem((NCH, 64, CW), BF16),
            vmem((NCH, 64, CW), BF16),
            vmem((NCH, 4, SH, CW), BF16),
            vmem((NCH, 4, 2 * SH, CW), BF16),
            dma((1,)),
            dma((2, HD)),
            dma((2,)),
            dma((NCH,)),
            dma((2 * CHIPS,)),
            dma((4,)),
            dma((NCTX,)),
            dma((2, 4)),
            dma((2, 4)),
            dma((NCTX,)),
            dma((NCTX,)),
            dma((NCTX,)),
            dma((NCTX,)),
            dma((NCTX,)),
            dma((NCTX,)),
            dma,
            dma,
            dma((CHIPS,)),
            dma((CHIPS,)),
            dma((CHIPS,)),
            dma((CHIPS,)),
            dma((CHIPS,)),
            dma((CHIPS,)),
            dma((NCH,)),
            dma((NCH,)),
            dma((NCH,)),
            dma((NCH,)),
            dma((NCH, 4)),
            dma((NCH, 4)),
        ],
        compiler_params=pltpu.CompilerParams(
            collective_id=0, has_side_effects=True, vmem_limit_bytes=60 * 1024 * 1024
        ),
        name="attention",
    )(
        span_latent.T,
        owner_rows,
        span_query,
        query_up,
        key_value_up,
        out_weight,
        step_query,
        latent_cache.reshape(ROWB * CPOS, KL + RD),
        cache_lengths,
    )
    return pl.pallas_call(
        place,
        out_shape=out_shape,
        in_specs=[in_vmem] * 2,
        out_specs=(in_vmem, in_vmem),
        name="place",
    )(*results)


def solution(mesh):
    in_specs = (
        P("ctx", None),
        P("ctx", None),
        P(None, "tp"),
        P(None, "tp"),
        P("tp", None),
        P("ctx"),
        P("ctx", None),
        P("ctx", "tp", None),
        P("ctx"),
    )
    out_specs = (P(("ctx", "tp"), None), P("ctx", "tp"))
    return jax.shard_map(body, mesh=mesh, in_specs=in_specs, out_specs=out_specs, check_vma=False)
```

```python
import math

import jax
import jax.numpy as jnp
from jax import lax
from jax.experimental import pallas as pl
from jax.experimental.pallas import tpu as pltpu
from jax.sharding import PartitionSpec as P

KL = 512
RD = 64
NOPE = 128
VD = 128
HD = 8
TOK = 256
LAT = 640
ROWB = 8
CPOS = 32
QL = 1536
D = 7168
NCTX = 8
NTP = 16
CHIPS = 8
NCH = 7
CW = D // NCH
SH = 16
NEGATIVE = -1e30
EXP_SCALE = (NOPE + RD) ** -0.5 * math.log2(math.e)
MESH = pl.DeviceIdType.MESH
F32 = jnp.float32
BF16 = jnp.bfloat16


def dot(a, b):
    return jnp.dot(a, b, preferred_element_type=F32)


def dot_t(a, b):
    return lax.dot_general(a, b, (((1,), (1,)), ((), ())), preferred_element_type=F32)


def iota(shape, dim):
    return lax.broadcasted_iota(jnp.int32, shape, dim)


def split_pair(y):
    rows = y.shape[0]
    low = iota((rows, 128), 1) < 64
    first, middle, last = y[:, :128], y[:, 128:256], y[:, 256:384]
    middle_turned = pltpu.roll(middle, 64, 1)
    last_turned = pltpu.roll(last, 64, 1)
    zero = jnp.zeros_like(first)
    return (
        (first, jnp.where(low, middle, zero)),
        (jnp.where(low, middle_turned, last_turned), jnp.where(low, last_turned, zero)),
    )


def kernel(
    lat_in, owner_in, xq_in, wq_in, kv_in, wo_in, sq_in, cache_in, len_in,
    out_ref, step_ref,
    lat_ref, owner_ref, sq_ref, len_ref, lat, ext, xq, wq, wk, wv, wv_t, wo, cache, q, run_max, run_sum, run_acc, head_out,
    keys, acc_send, acc_recv, ml_send, ml_recv,
    pair_send, own, pair_recv, stage, x_recv, x_sum, z_recv, zz_recv,
    load_sem, kv_sem, wq_sem, wo_sem, xq_sem,
    lat_s, lat_r, over_s, over_r, rel_s, rel_r, ext_s, ext_r, hand_s, hand_r, cache_s, cache_r, key_s, key_r,
    acc_s, acc_r, ml_s, ml_r, pair_s, pair_r, x_s, x_r, z_s, z_r,
):
    c = lax.axis_index("ctx")
    t = lax.axis_index("tp")
    core = t % 2
    chip = t // 2
    sibling = {"ctx": c, "tp": t + 1 - 2 * core}
    across = (t + CHIPS) % NTP
    opposite = (chip + 4) % CHIPS
    x_hi = chip // 4
    z = chip % 4
    x_lo = c // 4
    y = c % 4

    def remote(src, dst, send, recv, device):
        return pltpu.make_async_remote_copy(
            src_ref=src, dst_ref=dst, send_sem=send, recv_sem=recv, device_id=device, device_id_type=MESH
        )

    small_loads = [
        pltpu.make_async_copy(source, held, load_sem.at[1 + n])
        for n, (source, held) in enumerate(
            ((lat_in, lat_ref), (owner_in, owner_ref), (sq_in, sq_ref), (len_in, len_ref))
        )
    ]
    for load in small_loads:
        load.start()
    wq_loads = [
        pltpu.make_async_copy(wq_in.at[:, pl.ds(768 * n, 768)], wq.at[n], wq_sem.at[n]) for n in range(2)
    ]
    for load in wq_loads:
        load.start()

    barrier = pltpu.get_barrier_semaphore()
    for d in range(1, NCTX):
        pl.semaphore_signal(barrier, inc=1, device_id={"ctx": (c + d) % NCTX, "tp": t}, device_id_type=MESH)
    pl.semaphore_signal(barrier, inc=1, device_id={"ctx": (c + 4) % NCTX, "tp": across}, device_id_type=MESH)
    for d in range(1, CHIPS):
        pl.semaphore_signal(barrier, inc=1, device_id={"ctx": c, "tp": (t + 2 * d) % NTP}, device_id_type=MESH)
    pl.semaphore_signal(barrier, inc=1, device_id=sibling, device_id_type=MESH)

    for load in small_loads:
        load.wait()
    owner_row = jnp.broadcast_to(owner_ref[...].astype(F32).reshape(1, TOK), (LAT - KL - RD, TOK))
    owner_row = jnp.where(iota((LAT - KL - RD, TOK), 0) == 0, owner_row, 0.0)
    lat[c] = jnp.concatenate([lat_ref[...].astype(F32), owner_row], axis=0).T.astype(BF16)

    pl.semaphore_wait(barrier, NCTX - 1 + 1 + CHIPS - 1 + 1)

    half = pl.ds(pl.multiple_of(core * 128, 128), 128)
    other_half = pl.ds(pl.multiple_of((1 - core) * 128, 128), 128)
    quarters = [pl.ds(pl.multiple_of(core * 128 + 64 * n, 64), 64) for n in range(2)]
    handoff = pl.ds(pl.multiple_of(t * SH, SH), SH)

    def y_copy(block, target):
        return remote(
            lat.at[block, half], lat.at[block, half], lat_s.at[target], lat_r.at[block], {"ctx": 4 * x_lo + target, "tp": t}
        )

    def over_copy(block, n):
        return remote(
            lat.at[block, quarters[n]],
            lat.at[block, quarters[n]],
            over_s.at[n, block],
            over_r.at[n, block],
            {"ctx": 4 + y, "tp": (t, across)[n]},
        )

    def ext_copy(source, target):
        return remote(
            lat.at[c, handoff], ext.at[core, source], ext_s.at[target], ext_r.at[source], {"ctx": target, "tp": t}
        )

    def whole(source):
        return ((x_lo == 0) & (source < 4)) | ((x_lo == 1) & (source <= c))

    def ext_relay(source, whose):
        return remote(
            ext.at[whose, source], ext.at[whose, source], hand_s.at[source], hand_r.at[source], sibling
        )

    def cache_relay(whose):
        return remote(cache.at[whose], cache.at[whose], cache_s, cache_r, sibling)

    def relay_copy(source):
        return remote(lat.at[source, half], lat.at[source, half], rel_s.at[source], rel_r.at[source], sibling)

    def relay_arrival(source):
        return remote(
            lat.at[source, other_half], lat.at[source, other_half], rel_s.at[source], rel_r.at[source], sibling
        )

    @pl.when(x_lo == 0)
    def _():
        over_copy(c, 0).start()
        over_copy(c, 1).start()

    for d in (1, 3, 2):
        target = (y + d) % 4

        @pl.when((x_lo == 0) | (target > y))
        def _(target=target):
            y_copy(c, target).start()

    kv_loads = []
    for h in range(HD):
        for part, held in enumerate((wk, wv)):
            kv_loads.append(
                pltpu.make_async_copy(
                    kv_in.at[:, pl.ds(256 * h + 128 * part, 128)], held.at[:, pl.ds(128 * h, 128)], kv_sem.at[part, h]
                )
            )
    for load in kv_loads:
        load.start()
    xq_loads = []
    for part in range(2):
        for n in range(CHIPS):
            parity = 1 - core if part == 0 else core
            row = pl.multiple_of((2 * n + parity) * SH, SH)
            xq_loads.append(
                pltpu.make_async_copy(
                    xq_in.at[pl.ds(row, SH)], xq.at[pl.ds((part * CHIPS + n) * SH, SH)], xq_sem.at[part * CHIPS + n]
                )
            )
    for load in xq_loads:
        load.start()
    cache_load = pltpu.make_async_copy(cache_in, cache.at[core], load_sem.at[0])
    cache_load.start()


    def send_handoff(n, carry):
        @pl.when((x_lo == 1) & (n < c))
        def _():
            ext_copy(c, n).start()

        return carry

    cache_load.wait()
    cache_relay(core).start()

    for load in xq_loads:
        load.wait()
    xq[TOK:] = jnp.concatenate([sq_ref[...].astype(F32), jnp.zeros((ROWB, QL), F32)], axis=0).astype(BF16)
    nopes, ropes = [], []
    for n in range(2):
        wq_loads[n].wait()
        up = dot(xq[...], wq[n])
        for m in range(2):
            for e, (nope, rope) in enumerate(split_pair(up[:, 384 * m : 384 * (m + 1)])):
                q[4 * n + 2 * m + e, :128] = nope[:TOK].T.astype(BF16)
                q[4 * n + 2 * m + e, 128:] = rope[:TOK].T.astype(BF16)
                nopes.append(nope[TOK : TOK + ROWB])
                ropes.append(rope[TOK : TOK + ROWB])

    for load in kv_loads:
        load.wait()
    absorbed = jnp.concatenate(
        [dot_t(nopes[h].astype(BF16), wk[:, 128 * h : 128 * (h + 1)]) for h in range(HD)], axis=0
    )
    keys[chip, :, :KL] = absorbed.astype(BF16)
    keys[chip, :, KL:] = jnp.concatenate(ropes, axis=0).astype(BF16)

    def key_across(whose):
        return remote(keys.at[whose], keys.at[whose], key_s.at[0], key_r.at[whose], {"ctx": c, "tp": across})

    def key_copy(whose, d, sem):
        target = {"ctx": c, "tp": 8 * x_hi + 2 * ((z + d) % 4) + core}
        return remote(keys.at[whose], keys.at[whose], key_s.at[sem], key_r.at[whose], target)

    key_across(chip).start()
    for d in (1, 3, 2):
        key_copy(chip, d, d).start()
    lax.fori_loop(0, NCTX, send_handoff, 0)

    wo_loads = [
        pltpu.make_async_copy(wo_in.at[:, pl.ds(CW * n, CW)], wo.at[n], wo_sem.at[n]) for n in range(NCH)
    ]
    for load in wo_loads:
        load.start()

    def hand_on(d):
        @pl.when(x_lo == 0)
        def _():
            block = (y + d) % 4
            y_copy(block, y).wait_recv()
            over_copy(block, 0).start()
            over_copy(block, 1).start()

            relay_copy(block).start()

    hand_on(1)

    wv_t[...] = wv[...].T
    hand_on(3)

    column = iota((TOK, TOK), 1)
    parity = jnp.where(column < 128, 1 - core, core)
    position = ((column % 128) // SH) * (2 * SH) + parity * SH + column % SH
    visible = iota((TOK, TOK), 0) <= position

    def fold(block, first):
        latents = lat[block, :, :KL]
        rope = lat[block, :, KL:]
        key = dot(latents, wk[...]).astype(BF16)
        value = dot(wv_t[...], latents.T).astype(BF16)

        def score(h):
            return dot(jnp.concatenate([key[:, 128 * h : 128 * (h + 1)], rope], axis=1), q[h])

        def weigh(h, weights, shrink):
            added = dot(value[128 * h : 128 * (h + 1)], weights)
            if not first:
                added = added + (run_acc[h].reshape(VD // 8, 8, TOK) * shrink[None]).reshape(VD, TOK)
            run_acc[h] = added

        scores = {h: score(h) for h in range(2)}
        late = None
        for h in range(HD):
            if h + 2 < HD:
                scores[h + 2] = score(h + 2)
            if late is not None:
                weigh(*late)
            here = scores.pop(h)
            if first:
                here = jnp.where(visible, here, NEGATIVE)
            here = here.reshape(TOK // 8, 8, TOK)
            top = jnp.max(jnp.max(here, axis=0), axis=0, keepdims=True)
            shrink = None
            if first:
                top = jnp.broadcast_to(top, (8, TOK))
            else:
                old = run_max[h]
                top = jnp.maximum(old, top)
                shrink = jnp.exp2((old - top) * EXP_SCALE)
            raised = jnp.exp2((here - top[None]) * EXP_SCALE)
            total = jnp.sum(raised, axis=0)
            run_max[h] = top
            run_sum[h] = total if first else run_sum[h] * shrink + total
            late = (h, raised.reshape(TOK, TOK).astype(BF16), shrink)
        weigh(*late)

    def forward(block):
        @pl.when(block >= 4)
        def _():
            y_copy(block, y).wait_recv()

        @pl.when(block < 4)
        def _():
            over_copy(block, 0).wait_recv()
            over_copy(block, 1).wait_recv()

        relay_copy(block).start()

    def block_at(n):
        m = n - y - 1
        other_ring = (y + m + (m // 2) * (1 - 2 * (m % 2)) + 8) % 4
        return jnp.where((x_lo == 0) | (n <= y), c - n, other_ring)

    @pl.when(x_lo == 1)
    def _():
        forward(block_at(1))

    fold(c, True)

    early = (x_lo == 1) & (y >= 1)
    ahead = jnp.where(early, 2, 1)
    decode_turn = jnp.where(x_lo == 1, c + 1 - ahead, NCTX - 1)

    @pl.when(early)
    def _():
        forward(block_at(2))

    hand_on(2)
    key_across(opposite).wait_recv()
    for d in (1, 3, 2):
        key_copy(opposite, d, 3 + d).start()

    def relay_handoff():
        def one(n, carry):
            @pl.when(jnp.logical_not(whole(n)))
            def _():
                ext_copy(n, c).wait_recv()
                ext_relay(n, core).start()

            return carry

        lax.fori_loop(0, NCTX, one, 0)

    def decode():
        for side in range(2):
            for d in range(1, 4):
                whose = 4 * (x_hi if side == 0 else 1 - x_hi) + (z + d) % 4
                key_copy(whose, d, d).wait_recv()
        def gather(n, carry):
            @pl.when((x_lo == 0) & (n > c) & (n < 4))
            def _():
                relay_arrival(n).wait_recv()

            @pl.when(whole(n))
            def _():
                for whose in range(2):
                    ext[whose, n] = lat[n, pl.ds(pl.multiple_of((2 * chip + whose) * SH, SH), SH)]

            @pl.when(jnp.logical_not(whole(n)))
            def _():
                ext_relay(n, 1 - core).wait_recv()

            return carry

        lax.fori_loop(0, NCTX, gather, 0)
        cache_relay(1 - core).wait_recv()
        extra = ext[...].reshape(2 * NCTX * SH, LAT)
        cached = cache[...].reshape(2 * ROWB * CPOS, KL + RD)
        shape = (ROWB, 512)
        column = iota(shape, 1)
        length = jnp.zeros(shape, jnp.int32)
        for b in range(ROWB):
            length = jnp.where(column % 256 // CPOS == b, len_ref[b], length)
        place = (2 * chip + column // 256) * CPOS + column % CPOS
        in_cache = (column % 256 // CPOS == iota(shape, 0)) & (place < length)
        pick = jnp.where(iota((ROWB, 128), 1) == RD, 1.0, 0.0).astype(BF16)
        owner = dot_t(pick, extra[:, KL:])
        named = owner == (ROWB * c + iota((ROWB, 256), 0)).astype(F32)
        bias = jnp.concatenate(
            [jnp.where(in_cache, 0.0, NEGATIVE), jnp.where(named, 0.0, NEGATIVE)], axis=1
        ).astype(F32)
        lane = iota((64, 128), 1)
        sub = iota((64, 128), 0)

        def chunk(g):
            query = keys[4 * g : 4 * g + 4].reshape(256, LAT)
            scores = jnp.concatenate(
                [
                    dot_t(query[:, :KL], cached[:, :KL]) + dot_t(query[:, KL : KL + RD], cached[:, KL:]),
                    dot_t(query, extra),
                ],
                axis=1,
            )
            scores = (scores.reshape(32, ROWB, 768) * EXP_SCALE + bias[None]).reshape(256, 768)
            top = jnp.max(scores, axis=1, keepdims=True)
            raised = jnp.exp2(scores - top)
            total = jnp.sum(raised, axis=1, keepdims=True)
            weights = raised.astype(BF16)
            mixed = dot(weights[:, :512], cached[:, :KL]) + dot(weights[:, 512:], extra[:, :KL])
            acc_send[4 * g : 4 * g + 4] = mixed.astype(BF16).reshape(4, 64, KL)
            for n in range(4):
                rows = slice(64 * n, 64 * (n + 1))
                packed = jnp.where(lane == sub, top[rows], 0.0) + jnp.where(lane == sub + 64, total[rows], 0.0)
                ml_send[4 * g + n] = jnp.broadcast_to(jnp.sum(packed, axis=0, keepdims=True), (8, 128))

        for g in range(2):
            chunk(g)

        def send(d, carry):
            target = (chip + d) % CHIPS
            acc_copy(target).start()
            ml_copy(target).start()
            return carry

        lax.fori_loop(1, CHIPS, send, 0)
        acc_recv[chip] = acc_send[chip]
        ml_recv[chip] = ml_send[chip]

    def acc_copy(target):
        return remote(
            acc_send.at[target],
            acc_recv.at[chip],
            acc_s.at[target],
            acc_r.at[chip],
            {"ctx": c, "tp": 2 * target + core},
        )

    def ml_copy(target):
        return remote(
            ml_send.at[target], ml_recv.at[chip], ml_s.at[target], ml_r.at[chip], {"ctx": c, "tp": 2 * target + core}
        )

    def acc_arrival(source):
        return remote(acc_send.at[source], acc_recv.at[source], acc_s.at[source], acc_r.at[source], sibling)

    def ml_arrival(source):
        return remote(ml_send.at[source], ml_recv.at[source], ml_s.at[source], ml_r.at[source], sibling)

    def turn(n, carry):
        @pl.when(n == 3)
        def _():
            relay_handoff()

        @pl.when((n + ahead <= c) & (x_lo == 1))
        def _():
            forward(block_at(n + ahead))

        @pl.when((n <= c) & jnp.logical_not(early & (n == c)))
        def _():
            relay_arrival(block_at(n)).wait_recv()

        @pl.when(n == decode_turn)
        def _():
            @pl.when(early)
            def _():
                relay_arrival(block_at(c)).wait_recv()

            decode()

        @pl.when(n <= c)
        def _():
            fold(block_at(n), False)

        return carry

    lax.fori_loop(1, NCTX, turn, 0)

    for h in range(HD):
        total = jnp.sum(run_sum[h], axis=0, keepdims=True)
        head_out[:, 128 * h : 128 * (h + 1)] = (run_acc[h] / total).T.astype(BF16)

    def pair_copy(n):
        return remote(pair_send.at[n], pair_recv.at[n], pair_s.at[n], pair_r.at[n], sibling)

    here_rows = pl.ds(pl.multiple_of(x_hi * 64, 64), 64)
    there_rows = pl.ds(pl.multiple_of(64 - x_hi * 64, 64), 64)

    def row_block(index, count=SH):
        return pl.ds(pl.multiple_of(index * count, count), count)

    def z_device(other):
        return {"ctx": c, "tp": 8 * x_hi + 2 * other + core}

    def z_first(n):
        return n % 2 == 1

    def x_copy(n):
        return remote(stage.at[n, there_rows], x_recv.at[n], x_s.at[n], x_r.at[n], {"ctx": c, "tp": across})

    def z_copy(n, other):
        return remote(x_sum.at[n, row_block(other)], z_recv.at[n, z], z_s.at[n, other], z_r.at[n, z], z_device(other))

    def z_arrival(n, other):
        return remote(z_recv.at[n, other], z_recv.at[n, other], z_s.at[n, other], z_r.at[n, other], sibling)

    def first_z_copy(n, other):
        return remote(
            stage.at[n, row_block(other, 2 * SH)], zz_recv.at[n, z], z_s.at[n, other], z_r.at[n, z], z_device(other)
        )

    def first_z_arrival(n, other):
        return remote(zz_recv.at[n, other], zz_recv.at[n, other], z_s.at[n, other], z_r.at[n, other], sibling)

    def last_x_copy(n):
        return remote(
            x_sum.at[n, row_block(1 - x_hi)], x_recv.at[n, :SH], x_s.at[n], x_r.at[n], {"ctx": c, "tp": across}
        )

    def project(n):
        wo_load = pltpu.make_async_copy(wo_in.at[:, pl.ds(CW * n, CW)], wo.at[n], wo_sem.at[n])
        wo_load.wait()
        for m in range(CW // 256):
            columns = slice(256 * m, 256 * (m + 1))
            term = dot(head_out[...], wo[n, :, columns])
            pair_send[n, :, columns] = term[:128].astype(BF16)
            own[n, :, columns] = term[128:].astype(BF16)
        pair_copy(n).start()

    def add_core(n):
        pair_copy(n).wait_recv()
        both = (own[n].astype(F32) + pair_recv[n].astype(F32)).astype(BF16)

        @pl.when(jnp.logical_not(z_first(n)))
        def _():
            stage[n] = both
            x_copy(n).start()

        @pl.when(z_first(n))
        def _():
            for other in range(4):
                for side in range(2):
                    to, of = (2 * other + side) * SH, (4 * side + other) * SH
                    stage[n, to : to + SH] = both[of : of + SH]
            for d in (1, 3, 2):
                first_z_copy(n, (z + d) % 4).start()

    def add_chips(n):
        @pl.when(jnp.logical_not(z_first(n)))
        def _():
            x_copy(n).wait_recv()
            x_sum[n] = (stage[n, here_rows].astype(F32) + x_recv[n].astype(F32)).astype(BF16)
            for d in (1, 3, 2):
                z_copy(n, (z + d) % 4).start()
            z_recv[n, z] = x_sum[n, row_block(z)]

        @pl.when(z_first(n))
        def _():
            summed = stage[n, row_block(z, 2 * SH)].astype(F32)
            for d in (1, 3, 2):
                other = (z + d) % 4
                first_z_arrival(n, other).wait_recv()
                summed = summed + zz_recv[n, other].astype(F32)
            x_sum[n, : 2 * SH] = summed.astype(BF16)
            last_x_copy(n).start()

    def column_turn(n, carry):
        @pl.when(n < NCH)
        def _():
            project(n)

        @pl.when((n >= 1) & (n < NCH + 1))
        def _():
            add_core(n - 1)

        @pl.when(n >= 3)
        def _():
            add_chips(n - 3)

        return carry

    lax.fori_loop(0, NCH + 3, column_turn, 0)

    def merge_arrivals(d, carry):
        source = (chip + d) % CHIPS
        acc_arrival(source).wait_recv()
        ml_arrival(source).wait_recv()
        return carry

    lax.fori_loop(1, CHIPS, merge_arrivals, 0)
    lane = iota((64, 128), 1)
    sub = iota((64, 128), 0)
    tops, totals = [], []
    for s in range(CHIPS):
        packed = jnp.broadcast_to(ml_recv[s, 0:1, :], (64, 128))
        tops.append(jnp.sum(jnp.where(lane == sub, packed, 0.0), axis=1, keepdims=True))
        totals.append(jnp.sum(jnp.where(lane == sub + 64, packed, 0.0), axis=1, keepdims=True))
    top = tops[0]
    for s in range(1, CHIPS):
        top = jnp.maximum(top, tops[s])
    total = jnp.zeros((64, 1), F32)
    summed = jnp.zeros((64, KL), F32)
    for s in range(CHIPS):
        weight = jnp.exp2(tops[s] - top)
        total = total + totals[s] * weight
        summed = summed + acc_recv[s].astype(F32) * weight
    mixed = summed / total
    for h in range(HD):
        step_ref[:, 128 * h : 128 * (h + 1)] = dot(
            mixed[ROWB * h : ROWB * (h + 1)].astype(BF16), wv[:, 128 * h : 128 * (h + 1)]
        )

    def sum_z(n):
        for d in range(1, 4):
            z_arrival(n, (z + d) % 4).wait_recv()
        summed = z_recv[n, 0].astype(F32)
        for other in range(1, 4):
            summed = summed + z_recv[n, other].astype(F32)
        out_ref[:, CW * n : CW * (n + 1)] = summed

    def sum_x(n):
        last_x_copy(n).wait_recv()
        summed = x_sum[n, row_block(x_hi)].astype(F32) + x_recv[n, :SH].astype(F32)
        out_ref[:, CW * n : CW * (n + 1)] = summed

    for n in range(NCH):
        if z_first(n):
            sum_x(n)
        else:
            sum_z(n)

    def drain_ctx(n, carry):
        @pl.when((n != c) & whole(n))
        def _():
            relay_copy(n).wait_send()

        @pl.when((x_lo == 1) & (n < c))
        def _():
            ext_copy(c, n).wait_send()

        @pl.when(jnp.logical_not(whole(n)))
        def _():
            ext_relay(n, core).wait_send()

        @pl.when(n != chip)
        def _():
            acc_copy(n).wait_send()
            ml_copy(n).wait_send()

        return carry

    lax.fori_loop(0, NCTX, drain_ctx, 0)

    @pl.when(x_lo == 0)
    def _():
        for block in range(4):
            over_copy(block, 0).wait_send()
            over_copy(block, 1).wait_send()

    for d in (1, 3, 2):
        target = (y + d) % 4

        @pl.when((x_lo == 0) | (target > y))
        def _(target=target):
            y_copy(c, target).wait_send()

    key_across(chip).wait_send()
    for d in (1, 3, 2):
        key_copy(chip, d, d).wait_send()
        key_copy(opposite, d, 3 + d).wait_send()
    cache_relay(core).wait_send()

    def drain_columns(n, carry):
        pair_copy(n).wait_send()

        @pl.when(jnp.logical_not(z_first(n)))
        def _():
            x_copy(n).wait_send()
            for d in range(1, 4):
                z_copy(n, (z + d) % 4).wait_send()

        @pl.when(z_first(n))
        def _():
            last_x_copy(n).wait_send()
            for d in range(1, 4):
                first_z_copy(n, (z + d) % 4).wait_send()

        return carry

    lax.fori_loop(0, NCH, drain_columns, 0)


def place(span_in, step_in, span_out, step_out):
    span_out[...] = span_in[...]
    step_out[...] = step_in[...]


def body(
    span_query,
    span_latent,
    query_up,
    key_value_up,
    out_weight,
    owner_rows,
    step_query,
    latent_cache,
    cache_lengths,
):
    dma = pltpu.SemaphoreType.DMA
    vmem = pltpu.VMEM
    anywhere = pl.BlockSpec(memory_space=pl.ANY)
    in_vmem = pl.BlockSpec(memory_space=pltpu.VMEM)
    out_shape = (
        jax.ShapeDtypeStruct((SH, D), F32),
        jax.ShapeDtypeStruct((ROWB, HD * VD), F32),
    )
    results = pl.pallas_call(
        kernel,
        out_shape=out_shape,
        in_specs=[anywhere] * 9,
        out_specs=(in_vmem, in_vmem),
        scratch_shapes=[
            vmem((KL + RD, TOK), BF16),
            vmem((TOK,), jnp.int32),
            vmem((ROWB, QL), BF16),
            pltpu.SMEM((ROWB,), jnp.int32),
            vmem((NCTX, TOK, LAT), BF16),
            vmem((2, NCTX, SH, LAT), BF16),
            vmem((TOK + 2 * ROWB, QL), BF16),
            vmem((2, QL, 768), BF16),
            vmem((KL, HD * NOPE), BF16),
            vmem((KL, HD * VD), BF16),
            vmem((HD * VD, KL), BF16),
            vmem((NCH, HD * VD, CW), BF16),
            vmem((2, ROWB * CPOS, KL + RD), BF16),
            vmem((HD, TOK, 256), BF16),
            vmem((HD, 8, TOK), F32),
            vmem((HD, 8, TOK), F32),
            vmem((HD, VD, TOK), F32),
            vmem((TOK, HD * VD), BF16),
            vmem((CHIPS, 64, LAT), BF16),
            vmem((CHIPS, 64, KL), BF16),
            vmem((CHIPS, 64, KL), BF16),
            vmem((CHIPS, 8, 128), F32),
            vmem((CHIPS, 8, 128), F32),
            vmem((NCH, 128, CW), BF16),
            vmem((NCH, 128, CW), BF16),
            vmem((NCH, 128, CW), BF16),
            vmem((NCH, 128, CW), BF16),
            vmem((NCH, 64, CW), BF16),
            vmem((NCH, 64, CW), BF16),
            vmem((NCH, 4, SH, CW), BF16),
            vmem((NCH, 4, 2 * SH, CW), BF16),
            dma((5,)),
            dma((2, HD)),
            dma((2,)),
            dma((NCH,)),
            dma((2 * CHIPS,)),
            dma((4,)),
            dma((NCTX,)),
            dma((2, 4)),
            dma((2, 4)),
            dma((NCTX,)),
            dma((NCTX,)),
            dma((NCTX,)),
            dma((NCTX,)),
            dma((NCTX,)),
            dma((NCTX,)),
            dma,
            dma,
            dma((CHIPS,)),
            dma((CHIPS,)),
            dma((CHIPS,)),
            dma((CHIPS,)),
            dma((CHIPS,)),
            dma((CHIPS,)),
            dma((NCH,)),
            dma((NCH,)),
            dma((NCH,)),
            dma((NCH,)),
            dma((NCH, 4)),
            dma((NCH, 4)),
        ],
        compiler_params=pltpu.CompilerParams(
            collective_id=0, has_side_effects=True, vmem_limit_bytes=60 * 1024 * 1024
        ),
        name="attention",
    )(
        span_latent.T,
        owner_rows,
        span_query,
        query_up,
        key_value_up,
        out_weight,
        step_query,
        latent_cache.reshape(ROWB * CPOS, KL + RD),
        cache_lengths,
    )
    return pl.pallas_call(
        place,
        out_shape=out_shape,
        in_specs=[in_vmem] * 2,
        out_specs=(in_vmem, in_vmem),
        name="place",
    )(*results)


def solution(mesh):
    in_specs = (
        P("ctx", None),
        P("ctx", None),
        P(None, "tp"),
        P(None, "tp"),
        P("tp", None),
        P("ctx"),
        P("ctx", None),
        P("ctx", "tp", None),
        P("ctx"),
    )
    out_specs = (P(("ctx", "tp"), None), P("ctx", "tp"))
    return jax.shard_map(body, mesh=mesh, in_specs=in_specs, out_specs=out_specs, check_vma=False)
```

```python
import math

import jax
import jax.numpy as jnp
from jax import lax
from jax.experimental import pallas as pl
from jax.experimental.pallas import tpu as pltpu
from jax.sharding import PartitionSpec as P

KL = 512
RD = 64
NOPE = 128
VD = 128
HD = 8
TOK = 256
LAT = 640
ROWB = 8
CPOS = 32
QL = 1536
D = 7168
NCTX = 8
NTP = 16
CHIPS = 8
NCH = 7
CW = D // NCH
SH = 16
NEGATIVE = -1e30
EXP_SCALE = (NOPE + RD) ** -0.5 * math.log2(math.e)
MESH = pl.DeviceIdType.MESH
F32 = jnp.float32
BF16 = jnp.bfloat16


def dot(a, b):
    return jnp.dot(a, b, preferred_element_type=F32)


def dot_t(a, b):
    return lax.dot_general(a, b, (((1,), (1,)), ((), ())), preferred_element_type=F32)


def iota(shape, dim):
    return lax.broadcasted_iota(jnp.int32, shape, dim)


def split_pair(y):
    rows = y.shape[0]
    low = iota((rows, 128), 1) < 64
    first, middle, last = y[:, :128], y[:, 128:256], y[:, 256:384]
    middle_turned = pltpu.roll(middle, 64, 1)
    last_turned = pltpu.roll(last, 64, 1)
    zero = jnp.zeros_like(first)
    return (
        (first, jnp.where(low, middle, zero)),
        (jnp.where(low, middle_turned, last_turned), jnp.where(low, last_turned, zero)),
    )


def kernel(
    lat_in, owner_in, xq_in, wq_in, kv_in, wo_in, sq_in, cache_in, len_in,
    out_ref, step_ref,
    lat_ref, owner_ref, sq_ref, len_ref, lat, ext, xq, wq, wk, wv, wv_t, wo, cache, q, run_max, run_sum, run_acc, head_out,
    keys, acc_send, acc_recv, ml_send, ml_recv,
    pair_send, own, pair_recv, stage, x_recv, x_sum, z_recv, zz_recv,
    load_sem, kv_sem, wq_sem, wo_sem, xq_sem,
    lat_s, lat_r, over_s, over_r, rel_s, rel_r, ext_s, ext_r, hand_s, hand_r, cache_s, cache_r, key_s, key_r,
    acc_s, acc_r, ml_s, ml_r, pair_s, pair_r, x_s, x_r, z_s, z_r,
):
    c = lax.axis_index("ctx")
    t = lax.axis_index("tp")
    core = t % 2
    chip = t // 2
    sibling = {"ctx": c, "tp": t + 1 - 2 * core}
    across = (t + CHIPS) % NTP
    opposite = (chip + 4) % CHIPS
    x_hi = chip // 4
    z = chip % 4
    x_lo = c // 4
    y = c % 4

    def remote(src, dst, send, recv, device):
        return pltpu.make_async_remote_copy(
            src_ref=src, dst_ref=dst, send_sem=send, recv_sem=recv, device_id=device, device_id_type=MESH
        )

    small_loads = [
        pltpu.make_async_copy(source, held, load_sem.at[1 + n])
        for n, (source, held) in enumerate(
            ((lat_in, lat_ref), (owner_in, owner_ref), (sq_in, sq_ref), (len_in, len_ref))
        )
    ]
    for load in small_loads:
        load.start()
    wq_loads = [
        pltpu.make_async_copy(wq_in.at[:, pl.ds(768 * n, 768)], wq.at[n], wq_sem.at[n]) for n in range(2)
    ]
    for load in wq_loads:
        load.start()

    barrier = pltpu.get_barrier_semaphore()
    for d in range(1, NCTX):
        pl.semaphore_signal(barrier, inc=1, device_id={"ctx": (c + d) % NCTX, "tp": t}, device_id_type=MESH)
    pl.semaphore_signal(barrier, inc=1, device_id={"ctx": (c + 4) % NCTX, "tp": across}, device_id_type=MESH)
    for d in range(1, CHIPS):
        pl.semaphore_signal(barrier, inc=1, device_id={"ctx": c, "tp": (t + 2 * d) % NTP}, device_id_type=MESH)
    pl.semaphore_signal(barrier, inc=1, device_id=sibling, device_id_type=MESH)

    for load in small_loads:
        load.wait()
    owner_row = jnp.broadcast_to(owner_ref[...].astype(F32).reshape(1, TOK), (LAT - KL - RD, TOK))
    owner_row = jnp.where(iota((LAT - KL - RD, TOK), 0) == 0, owner_row, 0.0)
    lat[c] = jnp.concatenate([lat_ref[...].astype(F32), owner_row], axis=0).T.astype(BF16)

    pl.semaphore_wait(barrier, NCTX - 1 + 1 + CHIPS - 1 + 1)

    half = pl.ds(pl.multiple_of(core * 128, 128), 128)
    other_half = pl.ds(pl.multiple_of((1 - core) * 128, 128), 128)
    quarters = [pl.ds(pl.multiple_of(core * 128 + 64 * n, 64), 64) for n in range(2)]
    handoff = pl.ds(pl.multiple_of(t * SH, SH), SH)

    def y_copy(block, target):
        return remote(
            lat.at[block, half], lat.at[block, half], lat_s.at[target], lat_r.at[block], {"ctx": 4 * x_lo + target, "tp": t}
        )

    def over_copy(block, n):
        return remote(
            lat.at[block, quarters[n]],
            lat.at[block, quarters[n]],
            over_s.at[n, block],
            over_r.at[n, block],
            {"ctx": 4 + y, "tp": (t, across)[n]},
        )

    def ext_copy(source, target):
        return remote(
            lat.at[c, handoff], ext.at[core, source], ext_s.at[target], ext_r.at[source], {"ctx": target, "tp": t}
        )

    def whole(source):
        return ((x_lo == 0) & (source < 4)) | ((x_lo == 1) & (source <= c))

    def ext_relay(source, whose):
        return remote(
            ext.at[whose, source], ext.at[whose, source], hand_s.at[source], hand_r.at[source], sibling
        )

    def cache_relay(whose):
        return remote(cache.at[whose], cache.at[whose], cache_s, cache_r, sibling)

    def relay_copy(source):
        return remote(lat.at[source, half], lat.at[source, half], rel_s.at[source], rel_r.at[source], sibling)

    def relay_arrival(source):
        return remote(
            lat.at[source, other_half], lat.at[source, other_half], rel_s.at[source], rel_r.at[source], sibling
        )

    @pl.when(x_lo == 0)
    def _():
        over_copy(c, 0).start()
        over_copy(c, 1).start()

    for d in (1, 3, 2):
        target = (y + d) % 4

        @pl.when((x_lo == 0) | (target > y))
        def _(target=target):
            y_copy(c, target).start()

    kv_loads = []
    for h in range(HD):
        for part, held in enumerate((wk, wv)):
            kv_loads.append(
                pltpu.make_async_copy(
                    kv_in.at[:, pl.ds(256 * h + 128 * part, 128)], held.at[:, pl.ds(128 * h, 128)], kv_sem.at[part, h]
                )
            )
    for load in kv_loads:
        load.start()
    xq_loads = []
    for part in range(2):
        for n in range(CHIPS):
            parity = 1 - core if part == 0 else core
            row = pl.multiple_of((2 * n + parity) * SH, SH)
            xq_loads.append(
                pltpu.make_async_copy(
                    xq_in.at[pl.ds(row, SH)], xq.at[pl.ds((part * CHIPS + n) * SH, SH)], xq_sem.at[part * CHIPS + n]
                )
            )
    for load in xq_loads:
        load.start()
    cache_load = pltpu.make_async_copy(cache_in, cache.at[core], load_sem.at[0])
    cache_load.start()


    def send_handoff(n, carry):
        @pl.when((x_lo == 1) & (n < c))
        def _():
            ext_copy(c, n).start()

        return carry

    cache_load.wait()
    cache_relay(core).start()

    for load in xq_loads:
        load.wait()
    xq[TOK:] = jnp.concatenate([sq_ref[...].astype(F32), jnp.zeros((ROWB, QL), F32)], axis=0).astype(BF16)
    nopes, ropes = [], []
    for n in range(2):
        wq_loads[n].wait()
        up = dot(xq[...], wq[n])
        for m in range(2):
            for e, (nope, rope) in enumerate(split_pair(up[:, 384 * m : 384 * (m + 1)])):
                q[4 * n + 2 * m + e, :128] = nope[:TOK].T.astype(BF16)
                q[4 * n + 2 * m + e, 128:] = rope[:TOK].T.astype(BF16)
                nopes.append(nope[TOK : TOK + ROWB])
                ropes.append(rope[TOK : TOK + ROWB])

    for load in kv_loads:
        load.wait()
    absorbed = jnp.concatenate(
        [dot_t(nopes[h].astype(BF16), wk[:, 128 * h : 128 * (h + 1)]) for h in range(HD)], axis=0
    )
    keys[chip, :, :KL] = absorbed.astype(BF16)
    keys[chip, :, KL:] = jnp.concatenate(ropes, axis=0).astype(BF16)

    def key_across(whose):
        return remote(keys.at[whose], keys.at[whose], key_s.at[0], key_r.at[whose], {"ctx": c, "tp": across})

    def key_copy(whose, d, sem):
        target = {"ctx": c, "tp": 8 * x_hi + 2 * ((z + d) % 4) + core}
        return remote(keys.at[whose], keys.at[whose], key_s.at[sem], key_r.at[whose], target)

    key_across(chip).start()
    for d in (1, 3, 2):
        key_copy(chip, d, d).start()
    lax.fori_loop(0, NCTX, send_handoff, 0)

    wo_loads = [
        pltpu.make_async_copy(wo_in.at[:, pl.ds(CW * n, CW)], wo.at[n], wo_sem.at[n]) for n in range(NCH)
    ]
    for load in wo_loads:
        load.start()

    def hand_on(d):
        @pl.when(x_lo == 0)
        def _():
            block = (y + d) % 4
            y_copy(block, y).wait_recv()
            over_copy(block, 0).start()
            over_copy(block, 1).start()

            relay_copy(block).start()

    hand_on(1)

    wv_t[...] = wv[...].T
    hand_on(3)

    column = iota((TOK, TOK), 1)
    parity = jnp.where(column < 128, 1 - core, core)
    position = ((column % 128) // SH) * (2 * SH) + parity * SH + column % SH
    visible = iota((TOK, TOK), 0) <= position

    def fold(block, first):
        latents = lat[block, :, :KL]
        rope = lat[block, :, KL:]
        key = dot(latents, wk[...]).astype(BF16)
        value = dot(wv_t[...], latents.T).astype(BF16)

        def score(h):
            return dot(jnp.concatenate([key[:, 128 * h : 128 * (h + 1)], rope], axis=1), q[h])

        def weigh(h, weights, shrink):
            added = dot(value[128 * h : 128 * (h + 1)], weights)
            if not first:
                added = added + (run_acc[h].reshape(VD // 8, 8, TOK) * shrink[None]).reshape(VD, TOK)
            run_acc[h] = added

        scores = {h: score(h) for h in range(2)}
        late = None
        for h in range(HD):
            if h + 2 < HD:
                scores[h + 2] = score(h + 2)
            if late is not None:
                weigh(*late)
            here = scores.pop(h)
            if first:
                here = jnp.where(visible, here, NEGATIVE)
            here = here.reshape(TOK // 8, 8, TOK)
            top = jnp.max(jnp.max(here, axis=0), axis=0, keepdims=True)
            shrink = None
            if first:
                top = jnp.broadcast_to(top, (8, TOK))
            else:
                old = run_max[h]
                top = jnp.maximum(old, top)
                shrink = jnp.exp2((old - top) * EXP_SCALE)
            raised = jnp.exp2((here - top[None]) * EXP_SCALE)
            total = jnp.sum(raised, axis=0)
            run_max[h] = top
            run_sum[h] = total if first else run_sum[h] * shrink + total
            late = (h, raised.reshape(TOK, TOK).astype(BF16), shrink)
        weigh(*late)

    def forward(block):
        @pl.when(block >= 4)
        def _():
            y_copy(block, y).wait_recv()

        @pl.when(block < 4)
        def _():
            over_copy(block, 0).wait_recv()
            over_copy(block, 1).wait_recv()

        relay_copy(block).start()

    def block_at(n):
        m = n - y - 1
        other_ring = (y + m + (m // 2) * (1 - 2 * (m % 2)) + 8) % 4
        return jnp.where((x_lo == 0) | (n <= y), c - n, other_ring)

    @pl.when(x_lo == 1)
    def _():
        forward(block_at(1))

    fold(c, True)

    early = (x_lo == 1) & (y >= 1)
    ahead = jnp.where(early, 2, 1)
    decode_turn = jnp.where(x_lo == 1, c + 1 - ahead, NCTX - 1)

    @pl.when(early)
    def _():
        forward(block_at(2))

    hand_on(2)
    key_across(opposite).wait_recv()
    for d in (1, 3, 2):
        key_copy(opposite, d, 3 + d).start()

    def relay_handoff():
        def one(n, carry):
            @pl.when(jnp.logical_not(whole(n)))
            def _():
                ext_copy(n, c).wait_recv()
                ext_relay(n, core).start()

            return carry

        lax.fori_loop(0, NCTX, one, 0)

    def decode():
        for side in range(2):
            for d in range(1, 4):
                whose = 4 * (x_hi if side == 0 else 1 - x_hi) + (z + d) % 4
                key_copy(whose, d, d).wait_recv()
        def gather(n, carry):
            @pl.when((x_lo == 0) & (n > c) & (n < 4))
            def _():
                relay_arrival(n).wait_recv()

            @pl.when(whole(n))
            def _():
                for whose in range(2):
                    ext[whose, n] = lat[n, pl.ds(pl.multiple_of((2 * chip + whose) * SH, SH), SH)]

            @pl.when(jnp.logical_not(whole(n)))
            def _():
                ext_relay(n, 1 - core).wait_recv()

            return carry

        lax.fori_loop(0, NCTX, gather, 0)
        cache_relay(1 - core).wait_recv()
        extra = ext[...].reshape(2 * NCTX * SH, LAT)
        cached = cache[...].reshape(2 * ROWB * CPOS, KL + RD)
        shape = (ROWB, 512)
        column = iota(shape, 1)
        length = jnp.zeros(shape, jnp.int32)
        for b in range(ROWB):
            length = jnp.where(column % 256 // CPOS == b, len_ref[b], length)
        place = (2 * chip + column // 256) * CPOS + column % CPOS
        in_cache = (column % 256 // CPOS == iota(shape, 0)) & (place < length)
        pick = jnp.where(iota((ROWB, 128), 1) == RD, 1.0, 0.0).astype(BF16)
        owner = dot_t(pick, extra[:, KL:])
        named = owner == (ROWB * c + iota((ROWB, 256), 0)).astype(F32)
        bias = jnp.concatenate(
            [jnp.where(in_cache, 0.0, NEGATIVE), jnp.where(named, 0.0, NEGATIVE)], axis=1
        ).astype(F32)
        lane = iota((64, 128), 1)
        sub = iota((64, 128), 0)

        def chunk(g):
            query = keys[4 * g : 4 * g + 4].reshape(256, LAT)
            scores = jnp.concatenate(
                [
                    dot_t(query[:, :KL], cached[:, :KL]) + dot_t(query[:, KL : KL + RD], cached[:, KL:]),
                    dot_t(query, extra),
                ],
                axis=1,
            )
            scores = (scores.reshape(32, ROWB, 768) * EXP_SCALE + bias[None]).reshape(256, 768)
            top = jnp.max(scores, axis=1, keepdims=True)
            raised = jnp.exp2(scores - top)
            total = jnp.sum(raised, axis=1, keepdims=True)
            weights = raised.astype(BF16)
            mixed = dot(weights[:, :512], cached[:, :KL]) + dot(weights[:, 512:], extra[:, :KL])
            acc_send[4 * g : 4 * g + 4] = mixed.astype(BF16).reshape(4, 64, KL)
            for n in range(4):
                rows = slice(64 * n, 64 * (n + 1))
                packed = jnp.where(lane == sub, top[rows], 0.0) + jnp.where(lane == sub + 64, total[rows], 0.0)
                ml_send[4 * g + n] = jnp.broadcast_to(jnp.sum(packed, axis=0, keepdims=True), (8, 128))

        for g in range(2):
            chunk(g)

        def send(d, carry):
            target = (chip + d) % CHIPS
            acc_copy(target).start()
            ml_copy(target).start()
            return carry

        lax.fori_loop(1, CHIPS, send, 0)
        acc_recv[chip] = acc_send[chip]
        ml_recv[chip] = ml_send[chip]

    def acc_copy(target):
        return remote(
            acc_send.at[target],
            acc_recv.at[chip],
            acc_s.at[target],
            acc_r.at[chip],
            {"ctx": c, "tp": 2 * target + core},
        )

    def ml_copy(target):
        return remote(
            ml_send.at[target], ml_recv.at[chip], ml_s.at[target], ml_r.at[chip], {"ctx": c, "tp": 2 * target + core}
        )

    def acc_arrival(source):
        return remote(acc_send.at[source], acc_recv.at[source], acc_s.at[source], acc_r.at[source], sibling)

    def ml_arrival(source):
        return remote(ml_send.at[source], ml_recv.at[source], ml_s.at[source], ml_r.at[source], sibling)

    def turn(n, carry):
        @pl.when(n == 3)
        def _():
            relay_handoff()

        @pl.when((n + ahead <= c) & (x_lo == 1))
        def _():
            forward(block_at(n + ahead))

        @pl.when((n <= c) & jnp.logical_not(early & (n == c)))
        def _():
            relay_arrival(block_at(n)).wait_recv()

        @pl.when(n == decode_turn)
        def _():
            @pl.when(early)
            def _():
                relay_arrival(block_at(c)).wait_recv()

            decode()

        @pl.when(n <= c)
        def _():
            fold(block_at(n), False)

        return carry

    lax.fori_loop(1, NCTX, turn, 0)

    for h in range(HD):
        total = jnp.sum(run_sum[h], axis=0, keepdims=True)
        head_out[:, 128 * h : 128 * (h + 1)] = (run_acc[h] / total).T.astype(BF16)

    def pair_copy(n):
        return remote(pair_send.at[n], pair_recv.at[n], pair_s.at[n], pair_r.at[n], sibling)

    here_rows = pl.ds(pl.multiple_of(x_hi * 64, 64), 64)
    there_rows = pl.ds(pl.multiple_of(64 - x_hi * 64, 64), 64)

    def row_block(index, count=SH):
        return pl.ds(pl.multiple_of(index * count, count), count)

    def z_device(other):
        return {"ctx": c, "tp": 8 * x_hi + 2 * other + core}

    def z_first(n):
        return n % 2 == 1

    def x_copy(n):
        return remote(stage.at[n, there_rows], x_recv.at[n], x_s.at[n], x_r.at[n], {"ctx": c, "tp": across})

    def z_copy(n, other):
        return remote(x_sum.at[n, row_block(other)], z_recv.at[n, z], z_s.at[n, other], z_r.at[n, z], z_device(other))

    def z_arrival(n, other):
        return remote(z_recv.at[n, other], z_recv.at[n, other], z_s.at[n, other], z_r.at[n, other], sibling)

    def first_z_copy(n, other):
        return remote(
            stage.at[n, row_block(other, 2 * SH)], zz_recv.at[n, z], z_s.at[n, other], z_r.at[n, z], z_device(other)
        )

    def first_z_arrival(n, other):
        return remote(zz_recv.at[n, other], zz_recv.at[n, other], z_s.at[n, other], z_r.at[n, other], sibling)

    def last_x_copy(n):
        return remote(
            x_sum.at[n, row_block(1 - x_hi)], x_recv.at[n, :SH], x_s.at[n], x_r.at[n], {"ctx": c, "tp": across}
        )

    def project(n):
        wo_load = pltpu.make_async_copy(wo_in.at[:, pl.ds(CW * n, CW)], wo.at[n], wo_sem.at[n])
        wo_load.wait()
        for m in range(CW // 256):
            columns = slice(256 * m, 256 * (m + 1))
            term = dot(head_out[...], wo[n, :, columns])
            pair_send[n, :, columns] = term[:128].astype(BF16)
            own[n, :, columns] = term[128:].astype(BF16)
        pair_copy(n).start()

    def add_core(n):
        pair_copy(n).wait_recv()
        both = (own[n].astype(F32) + pair_recv[n].astype(F32)).astype(BF16)

        @pl.when(jnp.logical_not(z_first(n)))
        def _():
            stage[n] = both
            x_copy(n).start()

        @pl.when(z_first(n))
        def _():
            for other in range(4):
                for side in range(2):
                    to, of = (2 * other + side) * SH, (4 * side + other) * SH
                    stage[n, to : to + SH] = both[of : of + SH]
            for d in (1, 3, 2):
                first_z_copy(n, (z + d) % 4).start()

    def add_chips(n):
        @pl.when(jnp.logical_not(z_first(n)))
        def _():
            x_copy(n).wait_recv()
            x_sum[n] = (stage[n, here_rows].astype(F32) + x_recv[n].astype(F32)).astype(BF16)
            for d in (1, 3, 2):
                z_copy(n, (z + d) % 4).start()
            z_recv[n, z] = x_sum[n, row_block(z)]

        @pl.when(z_first(n))
        def _():
            summed = stage[n, row_block(z, 2 * SH)].astype(F32)
            for d in (1, 3, 2):
                other = (z + d) % 4
                first_z_arrival(n, other).wait_recv()
                summed = summed + zz_recv[n, other].astype(F32)
            x_sum[n, : 2 * SH] = summed.astype(BF16)
            last_x_copy(n).start()

    def column_turn(n, carry):
        @pl.when(n < NCH)
        def _():
            project(n)

        @pl.when((n >= 1) & (n < NCH + 1))
        def _():
            add_core(n - 1)

        @pl.when(n >= 4)
        def _():
            add_chips(n - 4)

        return carry

    lax.fori_loop(0, NCH + 4, column_turn, 0)

    def merge_arrivals(d, carry):
        source = (chip + d) % CHIPS
        acc_arrival(source).wait_recv()
        ml_arrival(source).wait_recv()
        return carry

    lax.fori_loop(1, CHIPS, merge_arrivals, 0)
    lane = iota((64, 128), 1)
    sub = iota((64, 128), 0)
    tops, totals = [], []
    for s in range(CHIPS):
        packed = jnp.broadcast_to(ml_recv[s, 0:1, :], (64, 128))
        tops.append(jnp.sum(jnp.where(lane == sub, packed, 0.0), axis=1, keepdims=True))
        totals.append(jnp.sum(jnp.where(lane == sub + 64, packed, 0.0), axis=1, keepdims=True))
    top = tops[0]
    for s in range(1, CHIPS):
        top = jnp.maximum(top, tops[s])
    total = jnp.zeros((64, 1), F32)
    summed = jnp.zeros((64, KL), F32)
    for s in range(CHIPS):
        weight = jnp.exp2(tops[s] - top)
        total = total + totals[s] * weight
        summed = summed + acc_recv[s].astype(F32) * weight
    mixed = summed / total
    for h in range(HD):
        step_ref[:, 128 * h : 128 * (h + 1)] = dot(
            mixed[ROWB * h : ROWB * (h + 1)].astype(BF16), wv[:, 128 * h : 128 * (h + 1)]
        )

    def sum_z(n):
        for d in range(1, 4):
            z_arrival(n, (z + d) % 4).wait_recv()
        summed = z_recv[n, 0].astype(F32)
        for other in range(1, 4):
            summed = summed + z_recv[n, other].astype(F32)
        out_ref[:, CW * n : CW * (n + 1)] = summed

    def sum_x(n):
        last_x_copy(n).wait_recv()
        summed = x_sum[n, row_block(x_hi)].astype(F32) + x_recv[n, :SH].astype(F32)
        out_ref[:, CW * n : CW * (n + 1)] = summed

    for n in range(NCH):
        if z_first(n):
            sum_x(n)
        else:
            sum_z(n)

    def drain_ctx(n, carry):
        @pl.when((n != c) & whole(n))
        def _():
            relay_copy(n).wait_send()

        @pl.when((x_lo == 1) & (n < c))
        def _():
            ext_copy(c, n).wait_send()

        @pl.when(jnp.logical_not(whole(n)))
        def _():
            ext_relay(n, core).wait_send()

        @pl.when(n != chip)
        def _():
            acc_copy(n).wait_send()
            ml_copy(n).wait_send()

        return carry

    lax.fori_loop(0, NCTX, drain_ctx, 0)

    @pl.when(x_lo == 0)
    def _():
        for block in range(4):
            over_copy(block, 0).wait_send()
            over_copy(block, 1).wait_send()

    for d in (1, 3, 2):
        target = (y + d) % 4

        @pl.when((x_lo == 0) | (target > y))
        def _(target=target):
            y_copy(c, target).wait_send()

    key_across(chip).wait_send()
    for d in (1, 3, 2):
        key_copy(chip, d, d).wait_send()
        key_copy(opposite, d, 3 + d).wait_send()
    cache_relay(core).wait_send()

    def drain_columns(n, carry):
        pair_copy(n).wait_send()

        @pl.when(jnp.logical_not(z_first(n)))
        def _():
            x_copy(n).wait_send()
            for d in range(1, 4):
                z_copy(n, (z + d) % 4).wait_send()

        @pl.when(z_first(n))
        def _():
            last_x_copy(n).wait_send()
            for d in range(1, 4):
                first_z_copy(n, (z + d) % 4).wait_send()

        return carry

    lax.fori_loop(0, NCH, drain_columns, 0)


def place(span_in, step_in, span_out, step_out):
    span_out[...] = span_in[...]
    step_out[...] = step_in[...]


def body(
    span_query,
    span_latent,
    query_up,
    key_value_up,
    out_weight,
    owner_rows,
    step_query,
    latent_cache,
    cache_lengths,
):
    dma = pltpu.SemaphoreType.DMA
    vmem = pltpu.VMEM
    anywhere = pl.BlockSpec(memory_space=pl.ANY)
    in_vmem = pl.BlockSpec(memory_space=pltpu.VMEM)
    out_shape = (
        jax.ShapeDtypeStruct((SH, D), F32),
        jax.ShapeDtypeStruct((ROWB, HD * VD), F32),
    )
    results = pl.pallas_call(
        kernel,
        out_shape=out_shape,
        in_specs=[anywhere] * 9,
        out_specs=(in_vmem, in_vmem),
        scratch_shapes=[
            vmem((KL + RD, TOK), BF16),
            vmem((TOK,), jnp.int32),
            vmem((ROWB, QL), BF16),
            pltpu.SMEM((ROWB,), jnp.int32),
            vmem((NCTX, TOK, LAT), BF16),
            vmem((2, NCTX, SH, LAT), BF16),
            vmem((TOK + 2 * ROWB, QL), BF16),
            vmem((2, QL, 768), BF16),
            vmem((KL, HD * NOPE), BF16),
            vmem((KL, HD * VD), BF16),
            vmem((HD * VD, KL), BF16),
            vmem((NCH, HD * VD, CW), BF16),
            vmem((2, ROWB * CPOS, KL + RD), BF16),
            vmem((HD, TOK, 256), BF16),
            vmem((HD, 8, TOK), F32),
            vmem((HD, 8, TOK), F32),
            vmem((HD, VD, TOK), F32),
            vmem((TOK, HD * VD), BF16),
            vmem((CHIPS, 64, LAT), BF16),
            vmem((CHIPS, 64, KL), BF16),
            vmem((CHIPS, 64, KL), BF16),
            vmem((CHIPS, 8, 128), F32),
            vmem((CHIPS, 8, 128), F32),
            vmem((NCH, 128, CW), BF16),
            vmem((NCH, 128, CW), BF16),
            vmem((NCH, 128, CW), BF16),
            vmem((NCH, 128, CW), BF16),
            vmem((NCH, 64, CW), BF16),
            vmem((NCH, 64, CW), BF16),
            vmem((NCH, 4, SH, CW), BF16),
            vmem((NCH, 4, 2 * SH, CW), BF16),
            dma((5,)),
            dma((2, HD)),
            dma((2,)),
            dma((NCH,)),
            dma((2 * CHIPS,)),
            dma((4,)),
            dma((NCTX,)),
            dma((2, 4)),
            dma((2, 4)),
            dma((NCTX,)),
            dma((NCTX,)),
            dma((NCTX,)),
            dma((NCTX,)),
            dma((NCTX,)),
            dma((NCTX,)),
            dma,
            dma,
            dma((CHIPS,)),
            dma((CHIPS,)),
            dma((CHIPS,)),
            dma((CHIPS,)),
            dma((CHIPS,)),
            dma((CHIPS,)),
            dma((NCH,)),
            dma((NCH,)),
            dma((NCH,)),
            dma((NCH,)),
            dma((NCH, 4)),
            dma((NCH, 4)),
        ],
        compiler_params=pltpu.CompilerParams(
            collective_id=0, has_side_effects=True, vmem_limit_bytes=60 * 1024 * 1024
        ),
        name="attention",
    )(
        span_latent.T,
        owner_rows,
        span_query,
        query_up,
        key_value_up,
        out_weight,
        step_query,
        latent_cache.reshape(ROWB * CPOS, KL + RD),
        cache_lengths,
    )
    return pl.pallas_call(
        place,
        out_shape=out_shape,
        in_specs=[in_vmem] * 2,
        out_specs=(in_vmem, in_vmem),
        name="place",
    )(*results)


def solution(mesh):
    in_specs = (
        P("ctx", None),
        P("ctx", None),
        P(None, "tp"),
        P(None, "tp"),
        P("tp", None),
        P("ctx"),
        P("ctx", None),
        P("ctx", "tp", None),
        P("ctx"),
    )
    out_specs = (P(("ctx", "tp"), None), P("ctx", "tp"))
    return jax.shard_map(body, mesh=mesh, in_specs=in_specs, out_specs=out_specs, check_vma=False)
```
